512 devices in a mesh: seq: 64 (over y, x, core), tp: 8 (over z).
Axes of the slice: x: 4, y: 8, z: 8, core: 2. Of those that a mesh axis runs over, the one named last changes fastest.
Arguments:
- byte_acts: bfloat16 [12288, 4096], P('seq', 'tp'), may hold values from -6 to 6
- upstream: bfloat16 [12288, 4096], P('seq', 'tp'), may hold values from -6 to 6
- segment_ids: int32 [12288], P('seq'), may hold values from 0 to 6143, never falling along the last dimension, each value on 1 to 40 neighbouring positions
- first_weight: bfloat16 [4096, 6144], P('seq', 'tp'), may hold values from -0.09375 to 0.09375
- second_weight: bfloat16 [4096, 6144], P('seq', 'tp'), may hold values from -0.078125 to 0.078125
Outputs:
- byte_grad: bfloat16 [12288, 4096], P('seq', 'tp')
The draws below stay inside these ranges and needn't reach their ends.
Inputs may be any that keep to these rules, and one draw needn't show every extreme that they name: `segment_ids`: segment numbers never fall along the bytes; every number is used; each segment holds 1 to 40 bytes, one exactly 40.
All inputs are finite; a program needn't handle non-finite values.
Results may differ from the reference program's by a relative error of at most 0.009.
Values may be sent and summed in bfloat16 or wider, within the bound.
No kernel may reach another device: no remote copies, remote signals or barrier semaphores. Data moves between devices by JAX's collectives and lax.ppermute only.
A program may use at most 64 MiB of HBM per device.

```python
import math
import jax
import jax.numpy as jnp
import numpy as np
from jax import lax

D = 4096
FF = 6144
SEGMAX = 40
TOKENS = 12288
NSEG = 6144
N_TP = 8


def levels(rng, extent, cuts, least, top_value):
    def one(dim, blocks):
        draws = jax.random.uniform(jax.random.fold_in(jax.random.fold_in(rng, 6), dim), (blocks,), jnp.float32, least / len(cuts), top_value / len(cuts))
        return jnp.repeat(jnp.exp(draws), extent[dim] // blocks).reshape((-1,) + (1,) * (len(extent) - dim - 1))

    loudness = one(*cuts[0])
    for cut in cuts[1:]:
        loudness = loudness * one(*cut)
    return loudness


def length_profile(number_of, total, reach, slope):
    loads = [(1 << 20) // math.isqrt(standing ** slope) + 1 for standing in range(2, number_of + 1)]
    spare, given = total - reach - (number_of - 1), [1] * (number_of - 1)
    while spare > 0:
        candidates = [i for i in range(number_of - 1) if given[i] < reach]
        whole, left = sum([loads[i] for i in candidates]), spare
        for i in candidates:
            addition = min(reach - given[i], max(1, left * loads[i] // whole), spare)
            given[i] = given[i] + addition
            spare = spare - addition
    return np.array([reach] + given)


def uneven(key, count, total, most, slope):
    if count == 2:
        one = jax.random.randint(key, (), max(1, total - most), min(most, total - 1) + 1)
        return jnp.stack([one, total - one])
    sizes = jnp.asarray(length_profile(count, total, most, slope), jnp.int32)
    pairs = (count - 1) // 2
    giver, taker = sizes[1:1 + 2 * pairs:2], sizes[2:2 + 2 * pairs:2]
    margin = jnp.minimum(giver - 1, most - taker)
    moved = jax.random.randint(jax.random.fold_in(key, 1), (pairs,), 0, 1 << 20) % (margin + 1)
    sizes = sizes.at[1:1 + 2 * pairs:2].set(giver - moved).at[2:2 + 2 * pairs:2].set(taker + moved)
    return sizes[jax.random.permutation(jax.random.fold_in(key, 2), count)]


def scatter_about(stream_key, extent, deviation, most, pieces=(), kind=jnp.bfloat16):
    gain = levels(stream_key, extent, pieces, -0.22, 0.18) if pieces else 1.0
    values = jax.random.normal(stream_key, extent, jnp.float32) * deviation * gain
    return jnp.minimum(jnp.maximum(values, -most), most).astype(kind)


def setup_inputs(seed: int = 0) -> dict:
    key_of = jax.random.split(jax.random.key(seed), 6)
    return {
        "byte_acts": scatter_about(key_of[0], (TOKENS, D), 1.0, 6.0, ((0, 64), (1, 8))),
        "upstream": scatter_about(key_of[1], (TOKENS, D), 1.0, 6.0, ((0, 64), (1, 8))),
        "segment_ids": jnp.searchsorted(jnp.cumsum(uneven(key_of[2], NSEG, TOKENS, SEGMAX, 2)), jnp.arange(TOKENS), side="right").astype(jnp.int32),
        "first_weight": scatter_about(key_of[3], (D, FF), D ** -0.5, 0.09375, ((0, 64), (1, 8))),
        "second_weight": scatter_about(key_of[4], (D, FF), FF ** -0.5, 0.078125, ((0, 64), (1, 8))),
    }


epsilon = 1e-06

def reference(byte_acts, upstream, segment_ids, first_weight, second_weight):
    ones = jnp.ones(segment_ids.shape, jnp.float32)
    counts = jax.ops.segment_sum(ones, segment_ids, num_segments=NSEG)
    seg_sums = jax.ops.segment_sum(byte_acts.astype(jnp.float32), segment_ids, num_segments=NSEG)
    pooled = seg_sums / counts[:, None]
    grad_sums = jax.ops.segment_sum(upstream.astype(jnp.float32), segment_ids, num_segments=NSEG)
    square_sums = lax.optimization_barrier(jnp.sum(pooled * pooled, axis=1))
    inv_rms = lax.rsqrt(square_sums / D + epsilon)
    normed = pooled * inv_rms[:, None]
    normed_b = normed.astype(jnp.bfloat16)
    grad_b = grad_sums.astype(jnp.bfloat16)
    up_proj = jnp.dot(normed_b, first_weight, preferred_element_type=jnp.float32)
    back_proj = jnp.dot(grad_b, second_weight, preferred_element_type=jnp.float32)
    sigmoid_up = jax.nn.sigmoid(up_proj)
    grad_hidden = (back_proj * sigmoid_up * (1.0 + up_proj * (1.0 - sigmoid_up))).astype(jnp.bfloat16)
    block_width = FF // N_TP
    norm_grad = jnp.zeros(pooled.shape, jnp.float32)
    for block in range(N_TP):
        hidden_part = grad_hidden[:, block * block_width:(block + 1) * block_width]
        weight_part = first_weight[:, block * block_width:(block + 1) * block_width]
        term = jnp.dot(hidden_part, weight_part.T, preferred_element_type=jnp.float32).astype(jnp.bfloat16)
        term = lax.optimization_barrier(term)
        norm_grad = norm_grad + term.astype(jnp.float32)
    norm_dot = lax.optimization_barrier(jnp.sum(norm_grad * normed, axis=1))
    pooled_grad = grad_sums + inv_rms[:, None] * (norm_grad - normed * (norm_dot / D)[:, None])
    byte_share = pooled_grad / counts[:, None]
    return (upstream.astype(jnp.float32) + byte_share[segment_ids]).astype(jnp.bfloat16)
```

```python
import jax
import jax.numpy as jnp
from jax import lax
from jax.sharding import PartitionSpec as P

epsilon = 1e-06


def shifted(shard, axis, by):
    count = lax.axis_size(axis)
    pairs = [(i, i + by) for i in range(count) if 0 <= i + by < count]
    return lax.ppermute(shard, axis, pairs)


def turned(shard, by):
    count = lax.axis_size("tp")
    return lax.ppermute(shard, "tp", [(i, (i + by) % count) for i in range(count)])


def ring_gather(block):
    count = lax.axis_size("tp")
    me = lax.axis_index("tp")
    rows, width = block.shape
    whole = jnp.zeros((rows, width * count), block.dtype)

    def put(whole, part, row, owner):
        return lax.dynamic_update_slice(whole, part, (row, lax.rem(owner + count, count) * width))

    whole = put(whole, block, 0, me)
    right = left = block
    for step in range(1, count // 2):
        right, left = turned(right, 1), turned(left, -1)
        whole = put(whole, right, 0, me - step)
        whole = put(whole, left, 0, me + step)
    half = rows // 2
    top, bottom = turned(right[:half], 1), turned(left[half:], -1)
    whole = put(whole, top, 0, me + count // 2)
    return put(whole, bottom, half, me + count // 2)


def body(byte_acts, upstream, segment_ids, first_weight, second_weight):
    byte_rows = segment_ids.shape[0]
    width = byte_acts.shape[1]
    hidden = first_weight.shape[1]
    model_width = width * lax.axis_size("tp")
    weights = lax.all_gather(
        jnp.concatenate([first_weight, second_weight], axis=1), "seq", axis=0, tiled=True
    )
    first_full, second_full = weights[:, :hidden], weights[:, hidden:]

    base_id = segment_ids[0]
    last_id = segment_ids[byte_rows - 1]
    slot_of = segment_ids - base_id
    slot_index = jnp.arange(byte_rows, dtype=jnp.int32)
    member = slot_index[:, None] == slot_of[None, :]
    member_b = member.astype(jnp.bfloat16)
    seg_sums = jnp.dot(member_b, byte_acts, preferred_element_type=jnp.float32)
    grad_sums = jnp.dot(member_b, upstream, preferred_element_type=jnp.float32)
    counts = jnp.sum(member.astype(jnp.float32), axis=1)

    last_slot = last_id - base_id

    def packed(slot, segment):
        at = lambda a: lax.dynamic_slice_in_dim(a, slot, 1, 0)
        tag = jnp.zeros((1, 128), jnp.float32) + (segment + 1).astype(jnp.float32)
        count = jnp.zeros((1, 128), jnp.float32) + at(counts)
        return jnp.concatenate([at(seg_sums), at(grad_sums), count, tag], axis=1)

    tail = shifted(packed(0, base_id), "seq", -1)
    head = shifted(packed(last_slot, last_id), "seq", 1)

    def pick(slot, segment, row):
        matched = row[0, 2 * width + 128] == (segment + 1).astype(jnp.float32)
        return ((slot_index == slot) & matched).astype(jnp.float32)

    tail_pick, head_pick = pick(last_slot, last_id, tail), pick(0, base_id, head)

    def joined(own, begin, end):
        return (
            own
            + tail_pick[:, None] * tail[:, begin:end]
            + head_pick[:, None] * head[:, begin:end]
        )

    seg_sums = joined(seg_sums, 0, width)
    grad_sums = joined(grad_sums, width, 2 * width)
    counts = counts + tail_pick * tail[0, 2 * width] + head_pick * head[0, 2 * width]
    safe_counts = jnp.maximum(counts, 1.0)
    pooled = seg_sums / safe_counts[:, None]

    gathered = ring_gather(
        jnp.concatenate([pooled.astype(jnp.bfloat16), grad_sums.astype(jnp.bfloat16)], axis=0)
    )
    pooled_b, grad_b = gathered[:byte_rows], gathered[byte_rows:]
    square_sums = jnp.sum(jnp.square(pooled_b.astype(jnp.float32)), axis=1)
    inv_rms = lax.rsqrt(square_sums / model_width + epsilon)[:, None]

    back_proj = jnp.dot(grad_b, second_full, preferred_element_type=jnp.float32)
    up_proj = inv_rms * jnp.dot(pooled_b, first_full, preferred_element_type=jnp.float32)
    sigmoid_up = jax.nn.sigmoid(up_proj)
    grad_hidden = (back_proj * sigmoid_up * (1.0 + up_proj * (1.0 - sigmoid_up))).astype(
        jnp.bfloat16
    )
    norm_dot = lax.psum(jnp.sum(grad_hidden.astype(jnp.float32) * up_proj, axis=1), "tp")
    partial_grad = lax.dot_general(
        grad_hidden, first_full, (((1,), (1,)), ((), ())), preferred_element_type=jnp.float32
    )
    norm_grad = lax.psum_scatter(
        partial_grad.astype(jnp.bfloat16), "tp", scatter_dimension=1, tiled=True
    ).astype(jnp.float32)
    normed = pooled * inv_rms
    pooled_grad = grad_sums + inv_rms * (
        norm_grad - normed * (norm_dot / model_width)[:, None]
    )
    byte_share = pooled_grad / safe_counts[:, None]
    spread = jnp.dot(
        member.astype(jnp.float32).T,
        byte_share,
        precision=lax.Precision.HIGHEST,
        preferred_element_type=jnp.float32,
    )
    return (upstream.astype(jnp.float32) + spread).astype(jnp.bfloat16)


def solution(mesh):
    return jax.shard_map(
        body,
        mesh=mesh,
        in_specs=(P("seq", "tp"), P("seq", "tp"), P("seq"), P("seq", "tp"), P("seq", "tp")),
        out_specs=P("seq", "tp"),
        check_vma=False,
    )
```

```python
import jax
import jax.numpy as jnp
from jax import lax
from jax.experimental import pallas as pl
from jax.experimental.pallas import tpu as pltpu
from jax.sharding import PartitionSpec as P

epsilon = 1e-06


def shifted(shard, axis, by):
    count = lax.axis_size(axis)
    pairs = [(i, i + by) for i in range(count) if 0 <= i + by < count]
    return lax.ppermute(shard, axis, pairs)


def turned(shard, by):
    count = lax.axis_size("tp")
    return lax.ppermute(shard, "tp", [(i, (i + by) % count) for i in range(count)])


def ring_gather(block):
    count = lax.axis_size("tp")
    me = lax.axis_index("tp")
    rows, width = block.shape
    whole = jnp.zeros((rows, width * count), block.dtype)

    def put(whole, part, row, owner):
        return lax.dynamic_update_slice(whole, part, (row, lax.rem(owner + count, count) * width))

    whole = put(whole, block, 0, me)
    right = left = block
    for step in range(1, count // 2):
        right, left = turned(right, 1), turned(left, -1)
        whole = put(whole, right, 0, me - step)
        whole = put(whole, left, 0, me + step)
    half = rows // 2
    top, bottom = turned(right[:half], 1), turned(left[half:], -1)
    whole = put(whole, top, 0, me + count // 2)
    return put(whole, bottom, half, me + count // 2)


def block_kernel(acts_ref, weights_ref, inv_rms_ref, out_ref, up_ref, back_ref, first_ref):
    step, steps = pl.program_id(0), pl.num_programs(0)
    rows, hidden = up_ref.shape

    @pl.when(step == 0)
    def _():
        up_ref[...] = jnp.zeros_like(up_ref)
        back_ref[...] = jnp.zeros_like(back_ref)

    first_ref[step] = weights_ref[:, :hidden]
    up_ref[...] += jnp.dot(
        acts_ref[:rows], weights_ref[:, :hidden], preferred_element_type=jnp.float32
    )
    back_ref[...] += jnp.dot(
        acts_ref[rows:], weights_ref[:, hidden:], preferred_element_type=jnp.float32
    )

    @pl.when(step == steps - 1)
    def _():
        up_proj = up_ref[...] * inv_rms_ref[...]
        sigmoid_up = jax.nn.sigmoid(up_proj)
        grad_hidden = (
            back_ref[...] * sigmoid_up * (1.0 + up_proj * (1.0 - sigmoid_up))
        ).astype(jnp.bfloat16)
        dots = lax.dot_general(
            jnp.ones((8, hidden), jnp.float32),
            grad_hidden.astype(jnp.float32) * up_proj,
            (((1,), (1,)), ((), ())),
            precision=lax.Precision.HIGHEST,
            preferred_element_type=jnp.float32,
        )
        high = dots.astype(jnp.bfloat16).astype(jnp.float32)
        extra = jnp.concatenate([high, dots - high], axis=0).astype(jnp.bfloat16)
        for block in range(out_ref.shape[0]):
            out_ref[block, :rows] = lax.dot_general(
                grad_hidden,
                first_ref[block],
                (((1,), (1,)), ((), ())),
                preferred_element_type=jnp.float32,
            ).astype(jnp.bfloat16)
            out_ref[block, rows:] = jnp.zeros((16, out_ref.shape[2]), jnp.bfloat16)
            out_ref[block, rows:, :rows] = extra


def block_terms(gathered, weights, inv_rms, width):
    rows, depth = gathered.shape[0] // 2, gathered.shape[1]
    hidden = weights.shape[1] // 2
    steps = depth // width
    return pl.pallas_call(
        block_kernel,
        grid=(steps,),
        in_specs=[
            pl.BlockSpec((2 * rows, width), lambda k: (0, k)),
            pl.BlockSpec((width, 2 * hidden), lambda k: (k, 0)),
            pl.BlockSpec((rows, 1), lambda k: (0, 0)),
        ],
        out_specs=pl.BlockSpec((steps, rows + 16, width), lambda k: (0, 0, 0)),
        out_shape=jax.ShapeDtypeStruct((steps, rows + 16, width), jnp.bfloat16),
        scratch_shapes=[
            pltpu.VMEM((rows, hidden), jnp.float32),
            pltpu.VMEM((rows, hidden), jnp.float32),
            pltpu.VMEM((steps, width, hidden), jnp.bfloat16),
        ],
        compiler_params=pltpu.CompilerParams(vmem_limit_bytes=40 * 1024 * 1024),
        cost_estimate=pl.CostEstimate(
            flops=6 * rows * depth * hidden,
            bytes_accessed=2 * (2 * rows * depth + 2 * depth * hidden + rows * depth),
            transcendentals=rows * hidden,
        ),
    )(gathered, weights, inv_rms)


def body(byte_acts, upstream, segment_ids, first_weight, second_weight):
    byte_rows = segment_ids.shape[0]
    width = byte_acts.shape[1]
    model_width = width * lax.axis_size("tp")
    weights = lax.all_gather(
        jnp.concatenate([first_weight, second_weight], axis=1), "seq", axis=0, tiled=True
    )
    base_id = segment_ids[0]
    last_id = segment_ids[byte_rows - 1]
    slot_of = segment_ids - base_id
    slot_index = jnp.arange(byte_rows, dtype=jnp.int32)
    member = slot_index[:, None] == slot_of[None, :]
    member_b = member.astype(jnp.bfloat16)
    seg_sums = jnp.dot(member_b, byte_acts, preferred_element_type=jnp.float32)
    grad_sums = jnp.dot(member_b, upstream, preferred_element_type=jnp.float32)
    counts = jnp.sum(member.astype(jnp.float32), axis=1)

    last_slot = last_id - base_id

    def packed(slot, segment):
        at = lambda a: lax.dynamic_slice_in_dim(a, slot, 1, 0)
        tag = jnp.zeros((1, 128), jnp.float32) + (segment + 1).astype(jnp.float32)
        count = jnp.zeros((1, 128), jnp.float32) + at(counts)
        return jnp.concatenate([at(seg_sums), at(grad_sums), count, tag], axis=1)

    tail = shifted(packed(0, base_id), "seq", -1)
    head = shifted(packed(last_slot, last_id), "seq", 1)

    def pick(slot, segment, row):
        matched = row[0, 2 * width + 128] == (segment + 1).astype(jnp.float32)
        return ((slot_index == slot) & matched).astype(jnp.float32)

    tail_pick, head_pick = pick(last_slot, last_id, tail), pick(0, base_id, head)

    def joined(own, begin, end):
        return (
            own
            + tail_pick[:, None] * tail[:, begin:end]
            + head_pick[:, None] * head[:, begin:end]
        )

    seg_sums = joined(seg_sums, 0, width)
    grad_sums = joined(grad_sums, width, 2 * width)
    counts = counts + tail_pick * tail[0, 2 * width] + head_pick * head[0, 2 * width]
    safe_counts = jnp.maximum(counts, 1.0)
    pooled = seg_sums / safe_counts[:, None]

    gathered = ring_gather(
        jnp.concatenate([pooled.astype(jnp.bfloat16), grad_sums.astype(jnp.bfloat16)], axis=0)
    )
    pooled_b = gathered[:byte_rows]
    square_sums = jnp.sum(jnp.square(pooled_b.astype(jnp.float32)), axis=1)
    inv_rms = lax.rsqrt(square_sums / model_width + epsilon)[:, None]

    sent = block_terms(gathered, weights, inv_rms, width)
    terms = lax.all_to_all(sent, "tp", split_axis=0, concat_axis=0, tiled=True).astype(jnp.float32)
    norm_grad = jnp.sum(terms[:, :byte_rows], axis=0)
    norm_dot = jnp.sum(terms[:, byte_rows, :byte_rows] + terms[:, byte_rows + 8, :byte_rows], axis=0)
    normed = pooled * inv_rms
    pooled_grad = grad_sums + inv_rms * (
        norm_grad - normed * (norm_dot / model_width)[:, None]
    )
    byte_share = pooled_grad / safe_counts[:, None]
    spread = jnp.dot(
        member.astype(jnp.float32).T,
        byte_share,
        precision=lax.Precision.HIGHEST,
        preferred_element_type=jnp.float32,
    )
    return (upstream.astype(jnp.float32) + spread).astype(jnp.bfloat16)


def solution(mesh):
    return jax.shard_map(
        body,
        mesh=mesh,
        in_specs=(P("seq", "tp"), P("seq", "tp"), P("seq"), P("seq", "tp"), P("seq", "tp")),
        out_specs=P("seq", "tp"),
        check_vma=False,
    )
```

```python
import jax
import jax.numpy as jnp
from jax import lax
from jax.experimental import pallas as pl
from jax.experimental.pallas import tpu as pltpu
from jax.sharding import PartitionSpec as P

epsilon = 1e-06


def shifted(shard, axis, by):
    count = lax.axis_size(axis)
    pairs = [(i, i + by) for i in range(count) if 0 <= i + by < count]
    return lax.ppermute(shard, axis, pairs)


def turned(shard, by):
    count = lax.axis_size("tp")
    return lax.ppermute(shard, "tp", [(i, (i + by) % count) for i in range(count)])


def ring_gather(block):
    count = lax.axis_size("tp")
    me = lax.axis_index("tp")
    rows, width = block.shape
    whole = jnp.zeros((rows, width * count), block.dtype)

    def put(whole, part, row, owner):
        return lax.dynamic_update_slice(whole, part, (row, lax.rem(owner + count, count) * width))

    whole = put(whole, block, 0, me)
    right = left = block
    for step in range(1, count // 2):
        right, left = turned(right, 1), turned(left, -1)
        whole = put(whole, right, 0, me - step)
        whole = put(whole, left, 0, me + step)
    half = rows // 2
    top, bottom = turned(right[:half], 1), turned(left[half:], -1)
    whole = put(whole, top, 0, me + count // 2)
    return put(whole, bottom, half, me + count // 2)


def block_kernel(acts_ref, weights_hbm, inv_rms_ref, out_ref, rest_ref, weights_ref, mixed_ref, sems):
    rows, depth = inv_rms_ref.shape[0], weights_ref.shape[0]
    hidden = weights_ref.shape[1] // 2
    blocks, kept, width = out_ref.shape
    chunk = depth // blocks
    copies = [
        pltpu.make_async_copy(
            weights_hbm.at[pl.ds(k * chunk, chunk)], weights_ref.at[pl.ds(k * chunk, chunk)], sems.at[k]
        )
        for k in range(blocks)
    ]
    for copy in copies:
        copy.start()
    up_proj = back_proj = jnp.zeros((rows, hidden), jnp.float32)
    for k, copy in enumerate(copies):
        copy.wait()
        at = pl.ds(k * chunk, chunk)
        up_proj += jnp.dot(
            acts_ref[:rows, at], weights_ref[at, :hidden], preferred_element_type=jnp.float32
        )
        back_proj += jnp.dot(
            acts_ref[rows:, at], weights_ref[at, hidden:], preferred_element_type=jnp.float32
        )
    up_proj = up_proj * inv_rms_ref[...]
    sigmoid_up = jax.nn.sigmoid(up_proj)
    grad_hidden = (back_proj * sigmoid_up * (1.0 + up_proj * (1.0 - sigmoid_up))).astype(
        jnp.bfloat16
    )
    dots = lax.dot_general(
        jnp.ones((4, hidden), jnp.float32),
        grad_hidden.astype(jnp.float32) * up_proj,
        (((1,), (1,)), ((), ())),
        precision=lax.Precision.HIGHEST,
        preferred_element_type=jnp.float32,
    )
    high = dots.astype(jnp.bfloat16).astype(jnp.float32)
    mixed_ref[...] = jnp.zeros_like(mixed_ref)
    mixed_ref[8:, :rows] = jnp.concatenate([high, dots - high], axis=0)
    even = kept - 16
    for block in range(blocks):
        term = lax.dot_general(
            grad_hidden,
            weights_ref[pl.ds(block * width, width), :hidden],
            (((1,), (1,)), ((), ())),
            preferred_element_type=jnp.float32,
        )
        mixed_ref[:8] = term[even : even + 8]
        out_ref[block, :even] = term[:even].astype(jnp.bfloat16)
        out_ref[block, even:] = mixed_ref[...].astype(jnp.bfloat16)
        rest_ref[block] = term[even:].astype(jnp.bfloat16)


def block_terms(gathered, weights, inv_rms, width, kept):
    rows, depth = gathered.shape[0] // 2, gathered.shape[1]
    hidden = weights.shape[1] // 2
    blocks = depth // width
    return pl.pallas_call(
        block_kernel,
        in_specs=[
            pl.BlockSpec(memory_space=pltpu.VMEM),
            pl.BlockSpec(memory_space=pl.ANY),
            pl.BlockSpec(memory_space=pltpu.VMEM),
        ],
        out_specs=[pl.BlockSpec(memory_space=pltpu.VMEM)] * 2,
        out_shape=[
            jax.ShapeDtypeStruct((blocks, kept, width), jnp.bfloat16),
            jax.ShapeDtypeStruct((blocks, rows - kept + 16, width), jnp.bfloat16),
        ],
        scratch_shapes=[
            pltpu.VMEM(weights.shape, jnp.bfloat16),
            pltpu.VMEM((16, width), jnp.float32),
            pltpu.SemaphoreType.DMA((blocks,)),
        ],
        compiler_params=pltpu.CompilerParams(vmem_limit_bytes=40 * 1024 * 1024),
        cost_estimate=pl.CostEstimate(
            flops=6 * rows * depth * hidden,
            bytes_accessed=2 * (2 * rows * depth + 2 * depth * hidden + rows * depth),
            transcendentals=rows * hidden,
        ),
    )(gathered, weights, inv_rms)


def body(byte_acts, upstream, segment_ids, first_weight, second_weight):
    byte_rows = segment_ids.shape[0]
    width = byte_acts.shape[1]
    model_width = width * lax.axis_size("tp")
    weights = lax.all_gather(
        jnp.concatenate([first_weight, second_weight], axis=1), "seq", axis=0, tiled=True
    )
    base_id = segment_ids[0]
    last_id = segment_ids[byte_rows - 1]
    slot_of = segment_ids - base_id
    slot_index = jnp.arange(byte_rows, dtype=jnp.int32)
    member = slot_index[:, None] == slot_of[None, :]
    member_b = member.astype(jnp.bfloat16)
    seg_sums = jnp.dot(member_b, byte_acts, preferred_element_type=jnp.float32)
    grad_sums = jnp.dot(member_b, upstream, preferred_element_type=jnp.float32)
    counts = jnp.sum(member.astype(jnp.float32), axis=1)

    last_slot = last_id - base_id

    def packed(slot, segment):
        at = lambda a: lax.dynamic_slice_in_dim(a, slot, 1, 0)
        tag = jnp.zeros((1, 128), jnp.float32) + (segment + 1).astype(jnp.float32)
        count = jnp.zeros((1, 128), jnp.float32) + at(counts)
        return jnp.concatenate([at(seg_sums), at(grad_sums), count, tag], axis=1)

    tail = shifted(packed(0, base_id), "seq", -1)
    head = shifted(packed(last_slot, last_id), "seq", 1)

    def pick(slot, segment, row):
        matched = row[0, 2 * width + 128] == (segment + 1).astype(jnp.float32)
        return ((slot_index == slot) & matched).astype(jnp.float32)

    tail_pick, head_pick = pick(last_slot, last_id, tail), pick(0, base_id, head)

    def joined(own, begin, end):
        return (
            own
            + tail_pick[:, None] * tail[:, begin:end]
            + head_pick[:, None] * head[:, begin:end]
        )

    seg_sums = joined(seg_sums, 0, width)
    grad_sums = joined(grad_sums, width, 2 * width)
    counts = counts + tail_pick * tail[0, 2 * width] + head_pick * head[0, 2 * width]
    safe_counts = jnp.maximum(counts, 1.0)
    pooled = seg_sums / safe_counts[:, None]

    gathered = ring_gather(
        jnp.concatenate([pooled.astype(jnp.bfloat16), grad_sums.astype(jnp.bfloat16)], axis=0)
    )
    pooled_b = gathered[:byte_rows]
    square_sums = jnp.sum(jnp.square(pooled_b.astype(jnp.float32)), axis=1)
    inv_rms = lax.rsqrt(square_sums / model_width + epsilon)[:, None]

    kept = 144
    sent, rest = block_terms(gathered, weights, inv_rms, width, kept)

    def exchanged(a):
        return lax.all_to_all(a, "tp", split_axis=0, concat_axis=0, tiled=True).astype(jnp.float32)

    terms = exchanged(sent)
    rest_grad = lax.cond(
        last_slot >= kept - 8,
        lambda a: jnp.sum(exchanged(a), axis=0)[8:],
        lambda a: jnp.zeros((byte_rows - kept + 8, width), jnp.float32),
        rest,
    )
    norm_grad = jnp.concatenate([jnp.sum(terms[:, : kept - 8], axis=0), rest_grad], axis=0)
    norm_dot = jnp.sum(
        terms[:, kept - 8, :byte_rows] + terms[:, kept - 4, :byte_rows], axis=0
    )
    normed = pooled * inv_rms
    pooled_grad = grad_sums + inv_rms * (
        norm_grad - normed * (norm_dot / model_width)[:, None]
    )
    byte_share = pooled_grad / safe_counts[:, None]
    spread = jnp.dot(
        member.astype(jnp.float32).T,
        byte_share,
        precision=lax.Precision.HIGHEST,
        preferred_element_type=jnp.float32,
    )
    return (upstream.astype(jnp.float32) + spread).astype(jnp.bfloat16)


def solution(mesh):
    return jax.shard_map(
        body,
        mesh=mesh,
        in_specs=(P("seq", "tp"), P("seq", "tp"), P("seq"), P("seq", "tp"), P("seq", "tp")),
        out_specs=P("seq", "tp"),
        check_vma=False,
    )
```

```python
import jax
import jax.numpy as jnp
from jax import lax
from jax.experimental import pallas as pl
from jax.experimental.pallas import tpu as pltpu
from jax.sharding import Mesh
from jax.sharding import PartitionSpec as P

epsilon = 1e-06
seq = ("y", "x", "core")
sizes = (8, 4, 2)


def shifted(shard, axis, by):
    count = lax.axis_size(axis)
    pairs = [(i, i + by) for i in range(count) if 0 <= i + by < count]
    return lax.ppermute(shard, axis, pairs)


def turned(shard, by):
    count = lax.axis_size("tp")
    return lax.ppermute(shard, "tp", [(i, (i + by) % count) for i in range(count)])


def ring_gather(block):
    count = lax.axis_size("tp")
    me = lax.axis_index("tp")
    rows, width = block.shape
    whole = jnp.zeros((rows, width * count), block.dtype)

    def put(whole, part, row, owner):
        return lax.dynamic_update_slice(whole, part, (row, lax.rem(owner + count, count) * width))

    whole = put(whole, block, 0, me)
    right = left = block
    for step in range(1, count // 2):
        right, left = turned(right, 1), turned(left, -1)
        whole = put(whole, right, 0, me - step)
        whole = put(whole, left, 0, me + step)
    half = rows // 2
    top, bottom = turned(right[:half], 1), turned(left[half:], -1)
    whole = put(whole, top, 0, me + count // 2)
    return put(whole, bottom, half, me + count // 2)


def block_kernel(acts_ref, weights_hbm, inv_rms_ref, out_ref, rest_ref, weights_ref, mixed_ref, sems):
    rows, depth = inv_rms_ref.shape[0], weights_ref.shape[0]
    hidden = weights_ref.shape[1] // 2
    blocks, kept, width = out_ref.shape
    chunk = depth // blocks
    count_y, count_x, count_core = sizes
    part = depth // (count_y * count_x * count_core)
    copies = []
    for y in range(count_y):
        for core in range(count_core):
            for x in range(count_x):
                there = ((y * count_core + core) * count_x + x) * part
                here = ((y * count_x + x) * count_core + core) * part
                copies.append(
                    pltpu.make_async_copy(
                        weights_hbm.at[pl.ds(there, part)],
                        weights_ref.at[pl.ds(here, part)],
                        sems.at[len(copies)],
                    )
                )
    for copy in copies:
        copy.start()
    per_chunk = len(copies) // blocks
    up_proj = back_proj = jnp.zeros((rows, hidden), jnp.float32)
    for k in range(blocks):
        for copy in copies[k * per_chunk : (k + 1) * per_chunk]:
            copy.wait()
        at = pl.ds(k * chunk, chunk)
        up_proj += jnp.dot(
            acts_ref[:rows, at], weights_ref[at, :hidden], preferred_element_type=jnp.float32
        )
        back_proj += jnp.dot(
            acts_ref[rows:, at], weights_ref[at, hidden:], preferred_element_type=jnp.float32
        )
    up_proj = up_proj * inv_rms_ref[...]
    sigmoid_up = jax.nn.sigmoid(up_proj)
    grad_hidden = (back_proj * sigmoid_up * (1.0 + up_proj * (1.0 - sigmoid_up))).astype(
        jnp.bfloat16
    )
    dots = lax.dot_general(
        jnp.ones((4, hidden), jnp.float32),
        grad_hidden.astype(jnp.float32) * up_proj,
        (((1,), (1,)), ((), ())),
        precision=lax.Precision.HIGHEST,
        preferred_element_type=jnp.float32,
    )
    high = dots.astype(jnp.bfloat16).astype(jnp.float32)
    mixed_ref[...] = jnp.zeros_like(mixed_ref)
    mixed_ref[8:, :rows] = jnp.concatenate([high, dots - high], axis=0)
    even = kept - 16
    for block in range(blocks):
        term = lax.dot_general(
            grad_hidden,
            weights_ref[pl.ds(block * width, width), :hidden],
            (((1,), (1,)), ((), ())),
            preferred_element_type=jnp.float32,
        )
        mixed_ref[:8] = term[even : even + 8]
        out_ref[block, :even] = term[:even].astype(jnp.bfloat16)
        out_ref[block, even:] = mixed_ref[...].astype(jnp.bfloat16)
        rest_ref[block] = term[even:].astype(jnp.bfloat16)


def block_terms(gathered, weights, inv_rms, width, kept):
    rows, depth = gathered.shape[0] // 2, gathered.shape[1]
    hidden = weights.shape[1] // 2
    blocks = depth // width
    return pl.pallas_call(
        block_kernel,
        in_specs=[
            pl.BlockSpec(memory_space=pltpu.VMEM),
            pl.BlockSpec(memory_space=pl.ANY),
            pl.BlockSpec(memory_space=pltpu.VMEM),
        ],
        out_specs=[pl.BlockSpec(memory_space=pltpu.VMEM)] * 2,
        out_shape=[
            pltpu.VMEM((blocks, kept, width), jnp.bfloat16),
            jax.ShapeDtypeStruct((blocks, rows - kept + 16, width), jnp.bfloat16),
        ],
        scratch_shapes=[
            pltpu.VMEM(weights.shape, jnp.bfloat16),
            pltpu.VMEM((16, width), jnp.float32),
            pltpu.SemaphoreType.DMA((sizes[0] * sizes[1] * sizes[2],)),
        ],
        compiler_params=pltpu.CompilerParams(vmem_limit_bytes=40 * 1024 * 1024),
        cost_estimate=pl.CostEstimate(
            flops=6 * rows * depth * hidden,
            bytes_accessed=2 * (2 * rows * depth + 2 * depth * hidden + rows * depth),
            transcendentals=rows * hidden,
        ),
    )(gathered, weights, inv_rms)


def body(byte_acts, upstream, segment_ids, first_weight, second_weight):
    byte_rows = segment_ids.shape[0]
    width = byte_acts.shape[1]
    model_width = width * lax.axis_size("tp")
    weights = jnp.concatenate([first_weight, second_weight], axis=1)
    weights = lax.all_gather(weights, "x", axis=0, tiled=True)
    weights = lax.all_gather(weights, ("y", "core"), axis=0, tiled=True)

    base_id = segment_ids[0]
    last_id = segment_ids[byte_rows - 1]
    slot_of = segment_ids - base_id
    slot_index = jnp.arange(byte_rows, dtype=jnp.int32)
    member = slot_index[:, None] == slot_of[None, :]
    member_b = member.astype(jnp.bfloat16)
    seg_sums = jnp.dot(member_b, byte_acts, preferred_element_type=jnp.float32)
    grad_sums = jnp.dot(member_b, upstream, preferred_element_type=jnp.float32)
    counts = jnp.sum(member.astype(jnp.float32), axis=1)

    last_slot = last_id - base_id

    def packed(slot, segment):
        at = lambda a: lax.dynamic_slice_in_dim(a, slot, 1, 0)
        tag = jnp.zeros((1, 128), jnp.float32) + (segment + 1).astype(jnp.float32)
        count = jnp.zeros((1, 128), jnp.float32) + at(counts)
        return jnp.concatenate([at(seg_sums), at(grad_sums), count, tag], axis=1)

    tail = shifted(packed(0, base_id), seq, -1)
    head = shifted(packed(last_slot, last_id), seq, 1)

    def pick(slot, segment, row):
        matched = row[0, 2 * width + 128] == (segment + 1).astype(jnp.float32)
        return ((slot_index == slot) & matched).astype(jnp.float32)

    tail_pick, head_pick = pick(last_slot, last_id, tail), pick(0, base_id, head)

    def joined(own, begin, end):
        return (
            own
            + tail_pick[:, None] * tail[:, begin:end]
            + head_pick[:, None] * head[:, begin:end]
        )

    seg_sums = joined(seg_sums, 0, width)
    grad_sums = joined(grad_sums, width, 2 * width)
    counts = counts + tail_pick * tail[0, 2 * width] + head_pick * head[0, 2 * width]
    safe_counts = jnp.maximum(counts, 1.0)
    pooled = seg_sums / safe_counts[:, None]

    gathered = ring_gather(
        jnp.concatenate([pooled.astype(jnp.bfloat16), grad_sums.astype(jnp.bfloat16)], axis=0)
    )
    pooled_b = gathered[:byte_rows]
    square_sums = jnp.sum(jnp.square(pooled_b.astype(jnp.float32)), axis=1)
    inv_rms = lax.rsqrt(square_sums / model_width + epsilon)[:, None]

    kept = 144
    sent, rest = block_terms(gathered, weights, inv_rms, width, kept)

    def exchanged(a):
        return lax.all_to_all(a, "tp", split_axis=0, concat_axis=0, tiled=True).astype(jnp.float32)

    terms = exchanged(sent)
    rest_grad = lax.cond(
        last_slot >= kept - 8,
        lambda a: jnp.sum(exchanged(a), axis=0)[8:],
        lambda a: jnp.zeros((byte_rows - kept + 8, width), jnp.float32),
        rest,
    )
    norm_grad = jnp.concatenate([jnp.sum(terms[:, : kept - 8], axis=0), rest_grad], axis=0)
    norm_dot = jnp.sum(
        terms[:, kept - 8, :byte_rows] + terms[:, kept - 4, :byte_rows], axis=0
    )
    normed = pooled * inv_rms
    pooled_grad = grad_sums + inv_rms * (
        norm_grad - normed * (norm_dot / model_width)[:, None]
    )
    byte_share = pooled_grad / safe_counts[:, None]
    spread = jnp.dot(
        member.astype(jnp.float32).T,
        byte_share,
        precision=lax.Precision.HIGHEST,
        preferred_element_type=jnp.float32,
    )
    return (upstream.astype(jnp.float32) + spread).astype(jnp.bfloat16)


def solution(mesh):
    grid = Mesh(mesh.devices.reshape(sizes + (-1,)), seq + ("tp",))
    return jax.shard_map(
        body,
        mesh=grid,
        in_specs=(P(seq, "tp"), P(seq, "tp"), P(seq), P(seq, "tp"), P(seq, "tp")),
        out_specs=P(seq, "tp"),
        check_vma=False,
    )
```

```python
import jax
import jax.numpy as jnp
from jax import lax
from jax.experimental import pallas as pl
from jax.experimental.pallas import tpu as pltpu
from jax.sharding import Mesh
from jax.sharding import PartitionSpec as P

epsilon = 1e-06
seq = ("y", "x", "core")
sizes = (8, 4, 2)


def shifted(shard, axis, by):
    count = lax.axis_size(axis)
    pairs = [(i, i + by) for i in range(count) if 0 <= i + by < count]
    return lax.ppermute(shard, axis, pairs)


def turned(shard, by):
    count = lax.axis_size("tp")
    return lax.ppermute(shard, "tp", [(i, (i + by) % count) for i in range(count)])


def ring_gather(block):
    count = lax.axis_size("tp")
    me = lax.axis_index("tp")
    rows, width = block.shape
    whole = jnp.zeros((rows, width * count), block.dtype)

    def put(whole, part, row, owner):
        return lax.dynamic_update_slice(whole, part, (row, lax.rem(owner + count, count) * width))

    whole = put(whole, block, 0, me)
    right = left = block
    for step in range(1, count // 2):
        right, left = turned(right, 1), turned(left, -1)
        whole = put(whole, right, 0, me - step)
        whole = put(whole, left, 0, me + step)
    half = rows // 2
    top, bottom = turned(right[:half], 1), turned(left[half:], -1)
    whole = put(whole, top, 0, me + count // 2)
    return put(whole, bottom, half, me + count // 2)


def block_kernel(acts_ref, weights_hbm, inv_rms_ref, out_ref, rest_ref, weights_ref, mixed_ref, sems):
    rows = inv_rms_ref.shape[0]
    hidden = weights_ref.shape[-1] // 2
    blocks, kept, width = out_ref.shape
    copies = [
        [
            pltpu.make_async_copy(
                weights_hbm.at[y, core], weights_ref.at[y, :, core], sems.at[y, core]
            )
            for core in range(weights_hbm.shape[1])
        ]
        for y in range(weights_hbm.shape[0])
    ]
    for pair in copies:
        for copy in pair:
            copy.start()
    per_chunk = len(copies) // blocks

    def chunk(k, columns):
        own = weights_ref[k * per_chunk : (k + 1) * per_chunk, :, :, :, columns]
        return own.reshape(width, hidden)

    first, second = slice(0, hidden), slice(hidden, 2 * hidden)
    up_proj = back_proj = jnp.zeros((rows, hidden), jnp.float32)
    for k in range(blocks):
        for pair in copies[k * per_chunk : (k + 1) * per_chunk]:
            for copy in pair:
                copy.wait()
        at = pl.ds(k * width, width)
        up_proj += jnp.dot(
            acts_ref[:rows, at], chunk(k, first), preferred_element_type=jnp.float32
        )
        back_proj += jnp.dot(
            acts_ref[rows:, at], chunk(k, second), preferred_element_type=jnp.float32
        )
    up_proj = up_proj * inv_rms_ref[...]
    sigmoid_up = jax.nn.sigmoid(up_proj)
    grad_hidden = (back_proj * sigmoid_up * (1.0 + up_proj * (1.0 - sigmoid_up))).astype(
        jnp.bfloat16
    )
    dots = lax.dot_general(
        jnp.ones((4, hidden), jnp.float32),
        grad_hidden.astype(jnp.float32) * up_proj,
        (((1,), (1,)), ((), ())),
        precision=lax.Precision.HIGHEST,
        preferred_element_type=jnp.float32,
    )
    high = dots.astype(jnp.bfloat16).astype(jnp.float32)
    mixed_ref[...] = jnp.zeros_like(mixed_ref)
    mixed_ref[8:, :rows] = jnp.concatenate([high, dots - high], axis=0)
    even = kept - 16
    for block in range(blocks):
        term = lax.dot_general(
            grad_hidden,
            chunk(block, first),
            (((1,), (1,)), ((), ())),
            preferred_element_type=jnp.float32,
        )
        mixed_ref[:8] = term[even : even + 8]
        out_ref[block, :even] = term[:even].astype(jnp.bfloat16)
        out_ref[block, even:] = mixed_ref[...].astype(jnp.bfloat16)
        rest_ref[block] = term[even:].astype(jnp.bfloat16)


def block_terms(gathered, weights, inv_rms, width, kept):
    rows, depth = gathered.shape[0] // 2, gathered.shape[1]
    hidden = weights.shape[1] // 2
    blocks = depth // width
    count_y, count_x, count_core = sizes
    part = depth // (count_y * count_x * count_core)
    return pl.pallas_call(
        block_kernel,
        in_specs=[
            pl.BlockSpec(memory_space=pltpu.VMEM),
            pl.BlockSpec(memory_space=pl.ANY),
            pl.BlockSpec(memory_space=pltpu.VMEM),
        ],
        out_specs=[pl.BlockSpec(memory_space=pltpu.VMEM)] * 2,
        out_shape=[
            pltpu.VMEM((blocks, kept, width), jnp.bfloat16),
            jax.ShapeDtypeStruct((blocks, rows - kept + 16, width), jnp.bfloat16),
        ],
        scratch_shapes=[
            pltpu.VMEM((count_y, count_x, count_core, part, 2 * hidden), jnp.bfloat16),
            pltpu.VMEM((16, width), jnp.float32),
            pltpu.SemaphoreType.DMA((count_y, count_core)),
        ],
        compiler_params=pltpu.CompilerParams(vmem_limit_bytes=40 * 1024 * 1024),
        cost_estimate=pl.CostEstimate(
            flops=6 * rows * depth * hidden,
            bytes_accessed=2 * (2 * rows * depth + 2 * depth * hidden + rows * depth),
            transcendentals=rows * hidden,
        ),
    )(gathered, weights.reshape(count_y, count_core, count_x, part, 2 * hidden), inv_rms)


def body(byte_acts, upstream, segment_ids, first_weight, second_weight):
    byte_rows = segment_ids.shape[0]
    width = byte_acts.shape[1]
    model_width = width * lax.axis_size("tp")
    weights = jnp.concatenate([first_weight, second_weight], axis=1)
    weights = lax.all_gather(weights, "x", axis=0, tiled=True)
    weights = lax.all_gather(weights, ("y", "core"), axis=0, tiled=True)

    base_id = segment_ids[0]
    last_id = segment_ids[byte_rows - 1]
    slot_of = segment_ids - base_id
    slot_index = jnp.arange(byte_rows, dtype=jnp.int32)
    member = slot_index[:, None] == slot_of[None, :]
    member_b = member.astype(jnp.bfloat16)
    seg_sums = jnp.dot(member_b, byte_acts, preferred_element_type=jnp.float32)
    grad_sums = jnp.dot(member_b, upstream, preferred_element_type=jnp.float32)
    counts = jnp.sum(member.astype(jnp.float32), axis=1)

    last_slot = last_id - base_id

    def packed(slot, segment):
        at = lambda a: lax.dynamic_slice_in_dim(a, slot, 1, 0)
        tag = jnp.zeros((1, 128), jnp.float32) + (segment + 1).astype(jnp.float32)
        count = jnp.zeros((1, 128), jnp.float32) + at(counts)
        return jnp.concatenate([at(seg_sums), at(grad_sums), count, tag], axis=1)

    tail = shifted(packed(0, base_id), seq, -1)
    head = shifted(packed(last_slot, last_id), seq, 1)

    def pick(slot, segment, row):
        matched = row[0, 2 * width + 128] == (segment + 1).astype(jnp.float32)
        return ((slot_index == slot) & matched).astype(jnp.float32)

    tail_pick, head_pick = pick(last_slot, last_id, tail), pick(0, base_id, head)

    def joined(own, begin, end):
        return (
            own
            + tail_pick[:, None] * tail[:, begin:end]
            + head_pick[:, None] * head[:, begin:end]
        )

    seg_sums = joined(seg_sums, 0, width)
    grad_sums = joined(grad_sums, width, 2 * width)
    counts = counts + tail_pick * tail[0, 2 * width] + head_pick * head[0, 2 * width]
    safe_counts = jnp.maximum(counts, 1.0)
    pooled = seg_sums / safe_counts[:, None]

    gathered = ring_gather(
        jnp.concatenate([pooled.astype(jnp.bfloat16), grad_sums.astype(jnp.bfloat16)], axis=0)
    )
    pooled_b = gathered[:byte_rows]
    square_sums = jnp.sum(jnp.square(pooled_b.astype(jnp.float32)), axis=1)
    inv_rms = lax.rsqrt(square_sums / model_width + epsilon)[:, None]

    kept = 144
    sent, rest = block_terms(gathered, weights, inv_rms, width, kept)

    def exchanged(a):
        return lax.all_to_all(a, "tp", split_axis=0, concat_axis=0, tiled=True).astype(jnp.float32)

    terms = lax.all_to_all(sent, "tp", split_axis=0, concat_axis=0, tiled=True)
    terms, rest = lax.optimization_barrier((terms, rest))
    terms = terms.astype(jnp.float32)
    rest_grad = lax.cond(
        last_slot >= kept - 8,
        lambda a: jnp.sum(exchanged(a), axis=0)[8:],
        lambda a: jnp.zeros((byte_rows - kept + 8, width), jnp.float32),
        rest,
    )
    norm_grad = jnp.concatenate([jnp.sum(terms[:, : kept - 8], axis=0), rest_grad], axis=0)
    norm_dot = jnp.sum(
        terms[:, kept - 8, :byte_rows] + terms[:, kept - 4, :byte_rows], axis=0
    )
    normed = pooled * inv_rms
    pooled_grad = grad_sums + inv_rms * (
        norm_grad - normed * (norm_dot / model_width)[:, None]
    )
    byte_share = pooled_grad / safe_counts[:, None]
    spread = jnp.dot(
        member.astype(jnp.float32).T,
        byte_share,
        precision=lax.Precision.HIGHEST,
        preferred_element_type=jnp.float32,
    )
    return (upstream.astype(jnp.float32) + spread).astype(jnp.bfloat16)


def solution(mesh):
    grid = Mesh(mesh.devices.reshape(sizes + (-1,)), seq + ("tp",))
    return jax.shard_map(
        body,
        mesh=grid,
        in_specs=(P(seq, "tp"), P(seq, "tp"), P(seq), P(seq, "tp"), P(seq, "tp")),
        out_specs=P(seq, "tp"),
        check_vma=False,
    )
```

```python
import functools

import jax
import jax.numpy as jnp
from jax import lax
from jax.experimental import pallas as pl
from jax.experimental.pallas import tpu as pltpu
from jax.sharding import Mesh
from jax.sharding import PartitionSpec as P

epsilon = 1e-06
seq = ("y", "x", "core")
sizes = (8, 4, 2)


def shifted(shard, axis, by):
    count = lax.axis_size(axis)
    pairs = [(i, i + by) for i in range(count) if 0 <= i + by < count]
    return lax.ppermute(shard, axis, pairs)


def turned(shard, by):
    count = lax.axis_size("tp")
    return lax.ppermute(shard, "tp", [(i, (i + by) % count) for i in range(count)])


def ring_gather(block):
    count = lax.axis_size("tp")
    me = lax.axis_index("tp")
    rows, width = block.shape
    whole = jnp.zeros((rows, width * count), block.dtype)

    def put(whole, part, row, owner):
        return lax.dynamic_update_slice(whole, part, (row, lax.rem(owner + count, count) * width))

    whole = put(whole, block, 0, me)
    right = left = block
    for step in range(1, count // 2):
        right, left = turned(right, 1), turned(left, -1)
        whole = put(whole, right, 0, me - step)
        whole = put(whole, left, 0, me + step)
    half = rows // 2
    top, bottom = turned(right[:half], 1), turned(left[half:], -1)
    whole = put(whole, top, 0, me + count // 2)
    return put(whole, bottom, half, me + count // 2)


def block_kernel(
    acts_ref, weights_hbm, inv_rms_ref, out_hbm, rest_hbm, weights_ref, mixed_ref, out_ref, rest_ref, sems, out_sems
):
    rows = inv_rms_ref.shape[0]
    hidden = weights_ref.shape[-1] // 2
    blocks, kept, width = out_ref.shape
    copies = [
        [
            pltpu.make_async_copy(
                weights_hbm.at[y, core], weights_ref.at[y, :, core], sems.at[y, core]
            )
            for core in range(weights_hbm.shape[1])
        ]
        for y in range(weights_hbm.shape[0])
    ]
    for pair in copies:
        for copy in pair:
            copy.start()
    per_chunk = len(copies) // blocks

    def chunk(k, columns):
        own = weights_ref[k * per_chunk : (k + 1) * per_chunk, :, :, :, columns]
        return own.reshape(width, hidden)

    first, second = slice(0, hidden), slice(hidden, 2 * hidden)
    up_proj = back_proj = jnp.zeros((rows, hidden), jnp.float32)
    for k in range(blocks):
        for pair in copies[k * per_chunk : (k + 1) * per_chunk]:
            for copy in pair:
                copy.wait()
        at = pl.ds(k * width, width)
        up_proj += jnp.dot(
            acts_ref[:rows, at], chunk(k, first), preferred_element_type=jnp.float32
        )
        back_proj += jnp.dot(
            acts_ref[rows:, at], chunk(k, second), preferred_element_type=jnp.float32
        )
    up_proj = up_proj * inv_rms_ref[...]
    sigmoid_up = jax.nn.sigmoid(up_proj)
    grad_hidden = (back_proj * sigmoid_up * (1.0 + up_proj * (1.0 - sigmoid_up))).astype(
        jnp.bfloat16
    )
    dots = lax.dot_general(
        jnp.ones((4, hidden), jnp.float32),
        grad_hidden.astype(jnp.float32) * up_proj,
        (((1,), (1,)), ((), ())),
        precision=lax.Precision.HIGHEST,
        preferred_element_type=jnp.float32,
    )
    high = dots.astype(jnp.bfloat16).astype(jnp.float32)
    mixed_ref[...] = jnp.zeros_like(mixed_ref)
    mixed_ref[8:, :rows] = jnp.concatenate([high, dots - high], axis=0)
    even = kept - 16
    results = []
    for block in range(blocks):
        term = lax.dot_general(
            grad_hidden,
            chunk(block, first),
            (((1,), (1,)), ((), ())),
            preferred_element_type=jnp.float32,
        )
        mixed_ref[:8] = term[even : even + 8]
        out_ref[block, :even] = term[:even].astype(jnp.bfloat16)
        out_ref[block, even:] = mixed_ref[...].astype(jnp.bfloat16)
        rest_ref[block] = term[even:].astype(jnp.bfloat16)
        results.append(pltpu.make_async_copy(out_ref.at[block], out_hbm.at[block], out_sems.at[0, block]))
        results.append(pltpu.make_async_copy(rest_ref.at[block], rest_hbm.at[block], out_sems.at[1, block]))
        results[-2].start()
        results[-1].start()
    for copy in results:
        copy.wait()


def block_terms(gathered, weights, inv_rms, width, kept):
    rows, depth = gathered.shape[0] // 2, gathered.shape[1]
    hidden = weights.shape[1] // 2
    blocks = depth // width
    count_y, count_x, count_core = sizes
    part = depth // (count_y * count_x * count_core)
    return pl.pallas_call(
        block_kernel,
        in_specs=[
            pl.BlockSpec(memory_space=pltpu.VMEM),
            pl.BlockSpec(memory_space=pl.ANY),
            pl.BlockSpec(memory_space=pltpu.VMEM),
        ],
        out_specs=[pl.BlockSpec(memory_space=pltpu.HBM)] * 2,
        out_shape=[
            jax.ShapeDtypeStruct((blocks, kept, width), jnp.bfloat16),
            jax.ShapeDtypeStruct((blocks, rows - kept + 16, width), jnp.bfloat16),
        ],
        scratch_shapes=[
            pltpu.VMEM((count_y, count_x, count_core, part, 2 * hidden), jnp.bfloat16),
            pltpu.VMEM((16, width), jnp.float32),
            pltpu.VMEM((blocks, kept, width), jnp.bfloat16),
            pltpu.VMEM((blocks, rows - kept + 16, width), jnp.bfloat16),
            pltpu.SemaphoreType.DMA((count_y, count_core)),
            pltpu.SemaphoreType.DMA((2, blocks)),
        ],
        compiler_params=pltpu.CompilerParams(vmem_limit_bytes=40 * 1024 * 1024),
        cost_estimate=pl.CostEstimate(
            flops=6 * rows * depth * hidden,
            bytes_accessed=2 * (2 * rows * depth + 2 * depth * hidden + rows * depth),
            transcendentals=rows * hidden,
        ),
    )(gathered, weights.reshape(count_y, count_core, count_x, part, 2 * hidden), inv_rms)


def sums_kernel(ids_ref, ids_row_ref, acts_ref, upstream_ref, seg_ref, grad_ref, count_ref, first_ref, last_ref):
    rows, width = acts_ref.shape
    base_id, last_id = ids_ref[0], ids_ref[rows - 1]
    slot = lax.broadcasted_iota(jnp.int32, (rows, rows), 0)
    member = (slot == ids_row_ref[...] - base_id).astype(jnp.float32)
    member_b = member.astype(jnp.bfloat16)
    seg_ref[...] = jnp.dot(member_b, acts_ref[...], preferred_element_type=jnp.float32)
    grad_ref[...] = jnp.dot(member_b, upstream_ref[...], preferred_element_type=jnp.float32)
    count_ref[...] = jnp.sum(member, axis=1, keepdims=True)
    for edge_ref, at, segment in ((first_ref, 0, base_id), (last_ref, last_id - base_id, last_id)):
        edge_ref[:, :width] = seg_ref[pl.ds(at, 1), :]
        edge_ref[:, width : 2 * width] = grad_ref[pl.ds(at, 1), :]
        count = jnp.sum(jnp.where(slot[:, :1] == at, count_ref[...], 0.0), axis=0, keepdims=True)
        edge_ref[:, 2 * width : 2 * width + 128] = jnp.broadcast_to(count, (1, 128))
        edge_ref[:, 2 * width + 128 :] = jnp.full((1, 128), (segment + 1).astype(jnp.float32))


def joined_kernel(
    ids_ref, seg_ref, grad_ref, count_ref, tail_ref, head_ref, both_ref, pooled_ref, sums_ref, safe_ref
):
    rows, width = seg_ref.shape
    base_id, last_id = ids_ref[0], ids_ref[rows - 1]
    slot = lax.broadcasted_iota(jnp.int32, (rows, 1), 0)

    def pick(edge_ref, at, segment):
        matched = edge_ref[:, 2 * width + 128 : 2 * width + 129] == (segment + 1).astype(jnp.float32)
        return jnp.where((slot == at) & matched, 1.0, 0.0)

    tail_pick = pick(tail_ref, last_id - base_id, last_id)
    head_pick = pick(head_ref, 0, base_id)

    def joined(own_ref, at):
        return own_ref[...] + tail_pick * tail_ref[:, at] + head_pick * head_ref[:, at]

    counts = joined(count_ref, slice(2 * width, 2 * width + 1))
    safe = jnp.maximum(counts, 1.0)
    pooled = joined(seg_ref, slice(0, width)) / safe
    sums = joined(grad_ref, slice(width, 2 * width))
    both_ref[:rows] = pooled.astype(jnp.bfloat16)
    both_ref[rows:] = sums.astype(jnp.bfloat16)
    pooled_ref[...] = pooled
    sums_ref[...] = sums
    safe_ref[...] = safe


def last_kernel(
    model_width,
    ids_ref,
    ids_column_ref,
    terms_ref,
    rest_ref,
    pooled_ref,
    sums_ref,
    safe_ref,
    inv_rms_ref,
    upstream_ref,
    out_ref,
    share_ref,
):
    rows = pooled_ref.shape[0]
    blocks, kept, _ = terms_ref.shape
    even = kept - 16
    norm_grad = terms_ref[0, :even].astype(jnp.float32)
    mixed = terms_ref[0, even:].astype(jnp.float32)
    for block in range(1, blocks):
        norm_grad += terms_ref[block, :even].astype(jnp.float32)
        mixed += terms_ref[block, even:].astype(jnp.float32)
    dots = mixed[8:9, :rows] + mixed[12:13, :rows]
    slot = lax.broadcasted_iota(jnp.int32, (rows, rows), 1)
    diagonal = lax.broadcasted_iota(jnp.int32, (rows, rows), 0) == slot
    norm_dot = jnp.sum(jnp.where(diagonal, dots, 0.0), axis=1, keepdims=True)

    def share(at, norm_grad):
        inv_rms = inv_rms_ref[at]
        normed = pooled_ref[at] * inv_rms
        mean = norm_dot[at] * (1.0 / model_width)
        pooled_grad = sums_ref[at] + inv_rms * (norm_grad - normed * mean)
        share_ref[at] = pooled_grad / safe_ref[at]

    share(slice(0, even), norm_grad)
    share(slice(even, even + 8), mixed[:8])
    share(slice(even + 8, rows), rest_ref[...])
    member = (slot == ids_column_ref[...] - ids_ref[0]).astype(jnp.float32).astype(jnp.bfloat16)
    left = share_ref[...]
    spread = upstream_ref[...].astype(jnp.float32)
    parts = []
    for _ in range(3):
        part = left.astype(jnp.bfloat16)
        left = left - part.astype(jnp.float32)
        parts.append(jnp.dot(member, part, preferred_element_type=jnp.float32))
    out_ref[...] = (spread + ((parts[2] + parts[1]) + parts[0])).astype(jnp.bfloat16)


def on_core(kernel, out_shape, *operands, scratch=()):
    vmem = pl.BlockSpec(memory_space=pltpu.VMEM)
    return pl.pallas_call(
        kernel,
        in_specs=[pl.BlockSpec(memory_space=pltpu.SMEM)] + [vmem] * (len(operands) - 1),
        out_specs=jax.tree.map(lambda _: vmem, out_shape),
        out_shape=out_shape,
        scratch_shapes=scratch,
        compiler_params=pltpu.CompilerParams(vmem_limit_bytes=24 * 1024 * 1024),
    )(*operands)


def body(byte_acts, upstream, segment_ids, first_weight, second_weight):
    byte_rows, width = byte_acts.shape
    model_width = width * lax.axis_size("tp")
    weights = jnp.concatenate([first_weight, second_weight], axis=1)
    weights = lax.all_gather(weights, "x", axis=0, tiled=True)
    weights = lax.all_gather(weights, ("y", "core"), axis=0, tiled=True)

    def array(rows, columns, dtype=jnp.float32):
        return jax.ShapeDtypeStruct((rows, columns), dtype)

    whole, column, edge = array(byte_rows, width), array(byte_rows, 1), array(1, 2 * width + 256)
    seg_sums, grad_sums, counts, first, last = on_core(
        sums_kernel,
        [whole, whole, column, edge, edge],
        segment_ids,
        segment_ids.reshape(1, byte_rows),
        byte_acts,
        upstream,
    )
    tail, head = shifted(first, seq, -1), shifted(last, seq, 1)
    both, pooled, grad_sums, safe_counts = on_core(
        joined_kernel,
        [array(2 * byte_rows, width, jnp.bfloat16), whole, whole, column],
        segment_ids,
        seg_sums,
        grad_sums,
        counts,
        tail,
        head,
    )
    gathered = ring_gather(both)
    pooled_b = gathered[:byte_rows]
    square_sums = jnp.sum(jnp.square(pooled_b.astype(jnp.float32)), axis=1)
    inv_rms = lax.rsqrt(square_sums / model_width + epsilon)[:, None]

    kept = 144
    sent, rest = block_terms(gathered, weights, inv_rms, width, kept)

    def exchanged(a):
        return lax.all_to_all(a, "tp", split_axis=0, concat_axis=0, tiled=True)

    terms, rest = lax.optimization_barrier((exchanged(sent), rest))
    rest_grad = lax.cond(
        segment_ids[byte_rows - 1] - segment_ids[0] >= kept - 8,
        lambda a: jnp.sum(exchanged(a).astype(jnp.float32), axis=0)[8:],
        lambda a: jnp.zeros((byte_rows - kept + 8, width), jnp.float32),
        rest,
    )
    return on_core(
        functools.partial(last_kernel, model_width),
        array(byte_rows, width, jnp.bfloat16),
        segment_ids,
        segment_ids.reshape(byte_rows, 1),
        terms,
        rest_grad,
        pooled,
        grad_sums,
        safe_counts,
        inv_rms,
        upstream,
        scratch=[pltpu.VMEM((byte_rows, width), jnp.float32)],
    )


def solution(mesh):
    grid = Mesh(mesh.devices.reshape(sizes + (-1,)), seq + ("tp",))
    return jax.shard_map(
        body,
        mesh=grid,
        in_specs=(P(seq, "tp"), P(seq, "tp"), P(seq), P(seq, "tp"), P(seq, "tp")),
        out_specs=P(seq, "tp"),
        check_vma=False,
    )
```

```python
import functools

import jax
import jax.numpy as jnp
from jax import lax
from jax.experimental import pallas as pl
from jax.experimental.pallas import tpu as pltpu
from jax.sharding import Mesh
from jax.sharding import PartitionSpec as P

epsilon = 1e-06
seq = ("y", "x", "core")
sizes = (8, 4, 2)


def shifted(shard, axis, by):
    count = lax.axis_size(axis)
    pairs = [(i, i + by) for i in range(count) if 0 <= i + by < count]
    return lax.ppermute(shard, axis, pairs)


def turned(shard, by):
    count = lax.axis_size("tp")
    return lax.ppermute(shard, "tp", [(i, (i + by) % count) for i in range(count)])


def ring_gather(block):
    count = lax.axis_size("tp")
    me = lax.axis_index("tp")
    rows, width = block.shape
    whole = jnp.zeros((rows, width * count), block.dtype)

    def put(whole, part, row, owner):
        return lax.dynamic_update_slice(whole, part, (row, lax.rem(owner + count, count) * width))

    whole = put(whole, block, 0, me)
    right = left = block
    for step in range(1, count // 2):
        right, left = turned(right, 1), turned(left, -1)
        whole = put(whole, right, 0, me - step)
        whole = put(whole, left, 0, me + step)
    half = rows // 2
    top, bottom = turned(right[:half], 1), turned(left[half:], -1)
    whole = put(whole, top, 0, me + count // 2)
    return put(whole, bottom, half, me + count // 2)


def block_kernel(
    acts_ref, weights_hbm, inv_rms_ref, out_hbm, rest_hbm, weights_ref, mixed_ref, out_ref, rest_ref, sems, out_sems
):
    rows = inv_rms_ref.shape[0]
    hidden = weights_ref.shape[-1] // 2
    blocks, kept, width = out_ref.shape
    copies = [
        [
            pltpu.make_async_copy(
                weights_hbm.at[y, core], weights_ref.at[y, :, core], sems.at[y, core]
            )
            for core in range(weights_hbm.shape[1])
        ]
        for y in range(weights_hbm.shape[0])
    ]
    for pair in copies:
        for copy in pair:
            copy.start()
    per_chunk = len(copies) // blocks

    def chunk(k, columns):
        own = weights_ref[k * per_chunk : (k + 1) * per_chunk, :, :, :, columns]
        return own.reshape(width, hidden)

    first, second = slice(0, hidden), slice(hidden, 2 * hidden)
    up_proj = back_proj = jnp.zeros((rows, hidden), jnp.float32)
    for k in range(blocks):
        for pair in copies[k * per_chunk : (k + 1) * per_chunk]:
            for copy in pair:
                copy.wait()
        at = pl.ds(k * width, width)
        up_proj += jnp.dot(
            acts_ref[:rows, at], chunk(k, first), preferred_element_type=jnp.float32
        )
        back_proj += jnp.dot(
            acts_ref[rows:, at], chunk(k, second), preferred_element_type=jnp.float32
        )
    up_proj = up_proj * inv_rms_ref[...]
    sigmoid_up = jax.nn.sigmoid(up_proj)
    grad_hidden = (back_proj * sigmoid_up * (1.0 + up_proj * (1.0 - sigmoid_up))).astype(
        jnp.bfloat16
    )
    dots = lax.dot_general(
        jnp.ones((4, hidden), jnp.float32),
        grad_hidden.astype(jnp.float32) * up_proj,
        (((1,), (1,)), ((), ())),
        precision=lax.Precision.HIGHEST,
        preferred_element_type=jnp.float32,
    )
    high = dots.astype(jnp.bfloat16).astype(jnp.float32)
    mixed_ref[...] = jnp.zeros_like(mixed_ref)
    mixed_ref[8:, :rows] = jnp.concatenate([high, dots - high], axis=0)
    even = kept - 16
    results = []
    for block in range(blocks):
        term = lax.dot_general(
            grad_hidden,
            chunk(block, first),
            (((1,), (1,)), ((), ())),
            preferred_element_type=jnp.float32,
        )
        mixed_ref[:8] = term[even : even + 8]
        out_ref[block, :even] = term[:even].astype(jnp.bfloat16)
        out_ref[block, even:] = mixed_ref[...].astype(jnp.bfloat16)
        rest_ref[block] = term[even:].astype(jnp.bfloat16)
        for i, (here, there) in enumerate(((out_ref, out_hbm), (rest_ref, rest_hbm))):
            results.append(pltpu.make_async_copy(here.at[block], there.at[block], out_sems.at[i, block]))
            results[-1].start()
    for copy in results:
        copy.wait()


def block_terms(gathered, weights, inv_rms, width, kept):
    rows, depth = gathered.shape[0] // 2, gathered.shape[1]
    hidden = weights.shape[1] // 2
    blocks = depth // width
    count_y, count_x, count_core = sizes
    part = depth // (count_y * count_x * count_core)
    return pl.pallas_call(
        block_kernel,
        in_specs=[
            pl.BlockSpec(memory_space=pltpu.VMEM),
            pl.BlockSpec(memory_space=pl.ANY),
            pl.BlockSpec(memory_space=pltpu.VMEM),
        ],
        out_specs=[pl.BlockSpec(memory_space=pltpu.HBM)] * 2,
        out_shape=[
            pltpu.HBM((blocks, kept, width), jnp.bfloat16),
            pltpu.HBM((blocks, rows - kept + 16, width), jnp.bfloat16),
        ],
        scratch_shapes=[
            pltpu.VMEM((count_y, count_x, count_core, part, 2 * hidden), jnp.bfloat16),
            pltpu.VMEM((16, width), jnp.float32),
            pltpu.VMEM((blocks, kept, width), jnp.bfloat16),
            pltpu.VMEM((blocks, rows - kept + 16, width), jnp.bfloat16),
            pltpu.SemaphoreType.DMA((count_y, count_core)),
            pltpu.SemaphoreType.DMA((2, blocks)),
        ],
        compiler_params=pltpu.CompilerParams(vmem_limit_bytes=40 * 1024 * 1024),
        cost_estimate=pl.CostEstimate(
            flops=6 * rows * depth * hidden,
            bytes_accessed=2 * (2 * rows * depth + 2 * depth * hidden + rows * depth),
            transcendentals=rows * hidden,
        ),
    )(gathered, weights.reshape(count_y, count_core, count_x, part, 2 * hidden), inv_rms)


def sums_kernel(ids_ref, ids_row_ref, acts_ref, upstream_ref, seg_ref, grad_ref, count_ref, first_ref, last_ref):
    rows, width = acts_ref.shape
    base_id, last_id = ids_ref[0], ids_ref[rows - 1]
    slot = lax.broadcasted_iota(jnp.int32, (rows, rows), 0)
    member = (slot == ids_row_ref[...] - base_id).astype(jnp.float32)
    member_b = member.astype(jnp.bfloat16)
    seg_ref[...] = jnp.dot(member_b, acts_ref[...], preferred_element_type=jnp.float32)
    grad_ref[...] = jnp.dot(member_b, upstream_ref[...], preferred_element_type=jnp.float32)
    count_ref[...] = jnp.sum(member, axis=1, keepdims=True)
    for edge_ref, at, segment in ((first_ref, 0, base_id), (last_ref, last_id - base_id, last_id)):
        edge_ref[:, :width] = seg_ref[pl.ds(at, 1), :]
        edge_ref[:, width : 2 * width] = grad_ref[pl.ds(at, 1), :]
        count = jnp.sum(jnp.where(slot[:, :1] == at, count_ref[...], 0.0), axis=0, keepdims=True)
        edge_ref[:, 2 * width : 2 * width + 128] = jnp.broadcast_to(count, (1, 128))
        edge_ref[:, 2 * width + 128 :] = jnp.full((1, 128), (segment + 1).astype(jnp.float32))


def joined_kernel(
    ids_ref, seg_ref, grad_ref, count_ref, tail_ref, head_ref, both_ref, pooled_ref, sums_ref, safe_ref
):
    rows, width = seg_ref.shape
    base_id, last_id = ids_ref[0], ids_ref[rows - 1]
    slot = lax.broadcasted_iota(jnp.int32, (rows, 1), 0)

    def pick(edge_ref, at, segment):
        matched = edge_ref[:, 2 * width + 128 : 2 * width + 129] == (segment + 1).astype(jnp.float32)
        return jnp.where((slot == at) & matched, 1.0, 0.0)

    tail_pick = pick(tail_ref, last_id - base_id, last_id)
    head_pick = pick(head_ref, 0, base_id)

    def joined(own_ref, at):
        return own_ref[...] + tail_pick * tail_ref[:, at] + head_pick * head_ref[:, at]

    counts = joined(count_ref, slice(2 * width, 2 * width + 1))
    safe = jnp.maximum(counts, 1.0)
    pooled = joined(seg_ref, slice(0, width)) / safe
    sums = joined(grad_ref, slice(width, 2 * width))
    both_ref[:rows] = pooled.astype(jnp.bfloat16)
    both_ref[rows:] = sums.astype(jnp.bfloat16)
    pooled_ref[...] = pooled
    sums_ref[...] = sums
    safe_ref[...] = safe


def last_kernel(
    model_width,
    ids_ref,
    ids_column_ref,
    terms_ref,
    rest_ref,
    pooled_ref,
    sums_ref,
    safe_ref,
    inv_rms_ref,
    upstream_ref,
    out_ref,
    share_ref,
):
    rows = pooled_ref.shape[0]
    blocks, kept, _ = terms_ref.shape
    even = kept - 16
    norm_grad = terms_ref[0, :even].astype(jnp.float32)
    mixed = terms_ref[0, even:].astype(jnp.float32)
    for block in range(1, blocks):
        norm_grad += terms_ref[block, :even].astype(jnp.float32)
        mixed += terms_ref[block, even:].astype(jnp.float32)
    dots = mixed[8:9, :rows] + mixed[12:13, :rows]
    slot = lax.broadcasted_iota(jnp.int32, (rows, rows), 1)
    diagonal = lax.broadcasted_iota(jnp.int32, (rows, rows), 0) == slot
    norm_dot = jnp.sum(jnp.where(diagonal, dots, 0.0), axis=1, keepdims=True)

    def share(at, norm_grad):
        inv_rms = inv_rms_ref[at]
        normed = pooled_ref[at] * inv_rms
        mean = norm_dot[at] * (1.0 / model_width)
        pooled_grad = sums_ref[at] + inv_rms * (norm_grad - normed * mean)
        share_ref[at] = pooled_grad / safe_ref[at]

    share(slice(0, even), norm_grad)
    share(slice(even, even + 8), mixed[:8])
    share(slice(even + 8, rows), rest_ref[...])
    member = (slot == ids_column_ref[...] - ids_ref[0]).astype(jnp.float32).astype(jnp.bfloat16)
    left = share_ref[...]
    spread = upstream_ref[...].astype(jnp.float32)
    parts = []
    for _ in range(3):
        part = left.astype(jnp.bfloat16)
        left = left - part.astype(jnp.float32)
        parts.append(jnp.dot(member, part, preferred_element_type=jnp.float32))
    out_ref[...] = (spread + ((parts[2] + parts[1]) + parts[0])).astype(jnp.bfloat16)


def on_core(kernel, out_shape, *operands, scratch=()):
    def whole(a):
        return pl.BlockSpec(a.shape, lambda i: (0,) * len(a.shape))

    return pl.pallas_call(
        kernel,
        grid=(1,),
        in_specs=[pl.BlockSpec(memory_space=pltpu.SMEM)] + [whole(a) for a in operands[1:]],
        out_specs=jax.tree.map(whole, out_shape),
        out_shape=out_shape,
        scratch_shapes=scratch,
        compiler_params=pltpu.CompilerParams(vmem_limit_bytes=24 * 1024 * 1024),
    )(*operands)


def body(byte_acts, upstream, segment_ids, first_weight, second_weight):
    byte_rows, width = byte_acts.shape
    model_width = width * lax.axis_size("tp")
    weights = jnp.concatenate([first_weight, second_weight], axis=1)
    weights = lax.all_gather(weights, "x", axis=0, tiled=True)
    weights = lax.all_gather(weights, ("y", "core"), axis=0, tiled=True)

    def array(rows, columns, dtype=jnp.float32):
        return jax.ShapeDtypeStruct((rows, columns), dtype)

    whole, column, edge = array(byte_rows, width), array(byte_rows, 1), array(1, 2 * width + 256)
    seg_sums, grad_sums, counts, first, last = on_core(
        sums_kernel,
        [whole, whole, column, edge, edge],
        segment_ids,
        segment_ids.reshape(1, byte_rows),
        byte_acts,
        upstream,
    )
    tail, head = shifted(first, seq, -1), shifted(last, seq, 1)
    both, pooled, grad_sums, safe_counts = on_core(
        joined_kernel,
        [array(2 * byte_rows, width, jnp.bfloat16), whole, whole, column],
        segment_ids,
        seg_sums,
        grad_sums,
        counts,
        tail,
        head,
    )
    gathered = ring_gather(both)
    pooled_b = gathered[:byte_rows]
    square_sums = jnp.sum(jnp.square(pooled_b.astype(jnp.float32)), axis=1)
    inv_rms = lax.rsqrt(square_sums / model_width + epsilon)[:, None]

    kept = 144
    sent, rest = block_terms(gathered, weights, inv_rms, width, kept)

    def exchanged(a):
        return lax.all_to_all(a, "tp", split_axis=0, concat_axis=0, tiled=True)

    terms, rest = lax.optimization_barrier((exchanged(sent), rest))
    rest_grad = lax.cond(
        segment_ids[byte_rows - 1] - segment_ids[0] >= kept - 8,
        lambda a: jnp.sum(exchanged(a).astype(jnp.float32), axis=0)[8:],
        lambda a: jnp.zeros((byte_rows - kept + 8, width), jnp.float32),
        rest,
    )
    return on_core(
        functools.partial(last_kernel, model_width),
        array(byte_rows, width, jnp.bfloat16),
        segment_ids,
        segment_ids.reshape(byte_rows, 1),
        terms,
        rest_grad,
        pooled,
        grad_sums,
        safe_counts,
        inv_rms,
        upstream,
        scratch=[pltpu.VMEM((byte_rows, width), jnp.float32)],
    )


def solution(mesh):
    grid = Mesh(mesh.devices.reshape(sizes + (-1,)), seq + ("tp",))
    return jax.shard_map(
        body,
        mesh=grid,
        in_specs=(P(seq, "tp"), P(seq, "tp"), P(seq), P(seq, "tp"), P(seq, "tp")),
        out_specs=P(seq, "tp"),
        check_vma=False,
    )
```

```python
import functools

import jax
import jax.numpy as jnp
from jax import lax
from jax.experimental import pallas as pl
from jax.experimental.pallas import tpu as pltpu
from jax.sharding import Mesh
from jax.sharding import PartitionSpec as P

epsilon = 1e-06
seq = ("y", "x", "core")
sizes = (8, 4, 2)


def shifted(shard, axis, by):
    count = lax.axis_size(axis)
    pairs = [(i, i + by) for i in range(count) if 0 <= i + by < count]
    return lax.ppermute(shard, axis, pairs)


def turned(shard, by):
    count = lax.axis_size("tp")
    return lax.ppermute(shard, "tp", [(i, (i + by) % count) for i in range(count)])


def ring_gather(block):
    count = lax.axis_size("tp")
    me = lax.axis_index("tp")
    rows, width = block.shape
    whole = jnp.zeros((rows, width * count), block.dtype)

    def put(whole, part, row, owner):
        return lax.dynamic_update_slice(whole, part, (row, lax.rem(owner + count, count) * width))

    whole = put(whole, block, 0, me)
    right = left = block
    for step in range(1, count // 2):
        right, left = turned(right, 1), turned(left, -1)
        whole = put(whole, right, 0, me - step)
        whole = put(whole, left, 0, me + step)
    half = rows // 2
    top, bottom = turned(right[:half], 1), turned(left[half:], -1)
    whole = put(whole, top, 0, me + count // 2)
    return put(whole, bottom, half, me + count // 2)


def block_kernel(
    acts_ref, weights_hbm, inv_rms_ref, out_hbm, rest_hbm, weights_ref, turned_ref, mixed_ref, out_ref, rest_ref, sems, out_sems
):
    rows = inv_rms_ref.shape[0]
    hidden = weights_ref.shape[-1] // 2
    blocks, kept, width = out_ref.shape
    copies = [
        [
            pltpu.make_async_copy(
                weights_hbm.at[y, core], weights_ref.at[y, :, core], sems.at[y, core]
            )
            for core in range(weights_hbm.shape[1])
        ]
        for y in range(weights_hbm.shape[0])
    ]
    for pair in copies:
        for copy in pair:
            copy.start()
    per_chunk = len(copies) // blocks

    def chunk(k, columns):
        own = weights_ref[k * per_chunk : (k + 1) * per_chunk, :, :, :, columns]
        return own.reshape(width, hidden)

    first, second = slice(0, hidden), slice(hidden, 2 * hidden)
    up_proj = back_proj = jnp.zeros((rows, hidden), jnp.float32)
    for k in range(blocks):
        for pair in copies[k * per_chunk : (k + 1) * per_chunk]:
            for copy in pair:
                copy.wait()
        at = pl.ds(k * width, width)
        own = chunk(k, first)
        up_proj += jnp.dot(acts_ref[:rows, at], own, preferred_element_type=jnp.float32)
        turned_ref[k] = own.T
        back_proj += jnp.dot(
            acts_ref[rows:, at], chunk(k, second), preferred_element_type=jnp.float32
        )
    up_proj = up_proj * inv_rms_ref[...]
    sigmoid_up = jax.nn.sigmoid(up_proj)
    grad_hidden = (back_proj * sigmoid_up * (1.0 + up_proj * (1.0 - sigmoid_up))).astype(
        jnp.bfloat16
    )
    dots = lax.dot_general(
        jnp.ones((4, hidden), jnp.float32),
        grad_hidden.astype(jnp.float32) * up_proj,
        (((1,), (1,)), ((), ())),
        precision=lax.Precision.HIGHEST,
        preferred_element_type=jnp.float32,
    )
    high = dots.astype(jnp.bfloat16).astype(jnp.float32)
    mixed_ref[...] = jnp.zeros_like(mixed_ref)
    mixed_ref[8:, :rows] = jnp.concatenate([high, dots - high], axis=0)
    even = kept - 16
    results = []
    for block in range(blocks):
        term = jnp.dot(grad_hidden, turned_ref[block], preferred_element_type=jnp.float32)
        mixed_ref[:8] = term[even : even + 8]
        out_ref[block, :even] = term[:even].astype(jnp.bfloat16)
        out_ref[block, even:] = mixed_ref[...].astype(jnp.bfloat16)
        rest_ref[block] = term[even:].astype(jnp.bfloat16)
        for i, (here, there) in enumerate(((out_ref, out_hbm), (rest_ref, rest_hbm))):
            results.append(pltpu.make_async_copy(here.at[block], there.at[block], out_sems.at[i, block]))
            results[-1].start()
    for copy in results:
        copy.wait()


def block_terms(gathered, weights, inv_rms, width, kept):
    rows, depth = gathered.shape[0] // 2, gathered.shape[1]
    hidden = weights.shape[1] // 2
    blocks = depth // width
    count_y, count_x, count_core = sizes
    part = depth // (count_y * count_x * count_core)
    return pl.pallas_call(
        block_kernel,
        in_specs=[
            pl.BlockSpec(memory_space=pltpu.VMEM),
            pl.BlockSpec(memory_space=pl.ANY),
            pl.BlockSpec(memory_space=pltpu.VMEM),
        ],
        out_specs=[pl.BlockSpec(memory_space=pltpu.HBM)] * 2,
        out_shape=[
            pltpu.HBM((blocks, kept, width), jnp.bfloat16),
            pltpu.HBM((blocks, rows - kept + 16, width), jnp.bfloat16),
        ],
        scratch_shapes=[
            pltpu.VMEM((count_y, count_x, count_core, part, 2 * hidden), jnp.bfloat16),
            pltpu.VMEM((blocks, hidden, width), jnp.bfloat16),
            pltpu.VMEM((16, width), jnp.float32),
            pltpu.VMEM((blocks, kept, width), jnp.bfloat16),
            pltpu.VMEM((blocks, rows - kept + 16, width), jnp.bfloat16),
            pltpu.SemaphoreType.DMA((count_y, count_core)),
            pltpu.SemaphoreType.DMA((2, blocks)),
        ],
        compiler_params=pltpu.CompilerParams(vmem_limit_bytes=40 * 1024 * 1024),
        cost_estimate=pl.CostEstimate(
            flops=6 * rows * depth * hidden,
            bytes_accessed=2 * (2 * rows * depth + 2 * depth * hidden + rows * depth),
            transcendentals=rows * hidden,
        ),
    )(gathered, weights.reshape(count_y, count_core, count_x, part, 2 * hidden), inv_rms)


def sums_kernel(ids_ref, ids_row_ref, acts_ref, upstream_ref, seg_ref, grad_ref, count_ref, first_ref, last_ref):
    rows, width = acts_ref.shape
    base_id, last_id = ids_ref[0], ids_ref[rows - 1]
    slot = lax.broadcasted_iota(jnp.int32, (rows, rows), 0)
    member = (slot == ids_row_ref[...] - base_id).astype(jnp.float32)
    member_b = member.astype(jnp.bfloat16)
    seg_ref[...] = jnp.dot(member_b, acts_ref[...], preferred_element_type=jnp.float32)
    grad_ref[...] = jnp.dot(member_b, upstream_ref[...], preferred_element_type=jnp.float32)
    count_ref[...] = jnp.sum(member, axis=1, keepdims=True)
    for edge_ref, at, segment in ((first_ref, 0, base_id), (last_ref, last_id - base_id, last_id)):
        edge_ref[:, :width] = seg_ref[pl.ds(at, 1), :]
        edge_ref[:, width : 2 * width] = grad_ref[pl.ds(at, 1), :]
        count = jnp.sum(jnp.where(slot[:, :1] == at, count_ref[...], 0.0), axis=0, keepdims=True)
        edge_ref[:, 2 * width : 2 * width + 128] = jnp.broadcast_to(count, (1, 128))
        edge_ref[:, 2 * width + 128 :] = jnp.full((1, 128), (segment + 1).astype(jnp.float32))


def joined_kernel(
    ids_ref, seg_ref, grad_ref, count_ref, tail_ref, head_ref, both_ref, pooled_ref, sums_ref, safe_ref
):
    rows, width = seg_ref.shape
    base_id, last_id = ids_ref[0], ids_ref[rows - 1]
    slot = lax.broadcasted_iota(jnp.int32, (rows, 1), 0)

    def pick(edge_ref, at, segment):
        matched = edge_ref[:, 2 * width + 128 : 2 * width + 129] == (segment + 1).astype(jnp.float32)
        return jnp.where((slot == at) & matched, 1.0, 0.0)

    tail_pick = pick(tail_ref, last_id - base_id, last_id)
    head_pick = pick(head_ref, 0, base_id)

    def joined(own_ref, at):
        return own_ref[...] + tail_pick * tail_ref[:, at] + head_pick * head_ref[:, at]

    counts = joined(count_ref, slice(2 * width, 2 * width + 1))
    safe = jnp.maximum(counts, 1.0)
    pooled = joined(seg_ref, slice(0, width)) / safe
    sums = joined(grad_ref, slice(width, 2 * width))
    both_ref[:rows] = pooled.astype(jnp.bfloat16)
    both_ref[rows:] = sums.astype(jnp.bfloat16)
    pooled_ref[...] = pooled
    sums_ref[...] = sums
    safe_ref[...] = safe


def last_kernel(
    model_width,
    ids_ref,
    ids_column_ref,
    terms_ref,
    rest_ref,
    pooled_ref,
    sums_ref,
    safe_ref,
    inv_rms_ref,
    upstream_ref,
    out_ref,
    share_ref,
):
    rows = pooled_ref.shape[0]
    blocks, kept, _ = terms_ref.shape
    even = kept - 16
    norm_grad = terms_ref[0, :even].astype(jnp.float32)
    mixed = terms_ref[0, even:].astype(jnp.float32)
    for block in range(1, blocks):
        norm_grad += terms_ref[block, :even].astype(jnp.float32)
        mixed += terms_ref[block, even:].astype(jnp.float32)
    dots = mixed[8:9, :rows] + mixed[12:13, :rows]
    slot = lax.broadcasted_iota(jnp.int32, (rows, rows), 1)
    diagonal = lax.broadcasted_iota(jnp.int32, (rows, rows), 0) == slot
    norm_dot = jnp.sum(jnp.where(diagonal, dots, 0.0), axis=1, keepdims=True)

    def share(at, norm_grad):
        inv_rms = inv_rms_ref[at]
        normed = pooled_ref[at] * inv_rms
        mean = norm_dot[at] * (1.0 / model_width)
        pooled_grad = sums_ref[at] + inv_rms * (norm_grad - normed * mean)
        share_ref[at] = pooled_grad / safe_ref[at]

    share(slice(0, even), norm_grad)
    share(slice(even, even + 8), mixed[:8])
    share(slice(even + 8, rows), rest_ref[...])
    member = (slot == ids_column_ref[...] - ids_ref[0]).astype(jnp.float32).astype(jnp.bfloat16)
    left = share_ref[...]
    spread = upstream_ref[...].astype(jnp.float32)
    parts = []
    for _ in range(2):
        part = left.astype(jnp.bfloat16)
        left = left - part.astype(jnp.float32)
        parts.append(jnp.dot(member, part, preferred_element_type=jnp.float32))
    out_ref[...] = (spread + (parts[1] + parts[0])).astype(jnp.bfloat16)


def on_core(kernel, out_shape, *operands, scratch=()):
    def whole(a):
        return pl.BlockSpec(a.shape, lambda i: (0,) * len(a.shape))

    return pl.pallas_call(
        kernel,
        grid=(1,),
        in_specs=[pl.BlockSpec(memory_space=pltpu.SMEM)] + [whole(a) for a in operands[1:]],
        out_specs=jax.tree.map(whole, out_shape),
        out_shape=out_shape,
        scratch_shapes=scratch,
        compiler_params=pltpu.CompilerParams(vmem_limit_bytes=24 * 1024 * 1024),
    )(*operands)


def body(byte_acts, upstream, segment_ids, first_weight, second_weight):
    byte_rows, width = byte_acts.shape
    model_width = width * lax.axis_size("tp")
    weights = jnp.concatenate([first_weight, second_weight], axis=1)
    weights = lax.all_gather(weights, "x", axis=0, tiled=True)
    weights = lax.all_gather(weights, ("y", "core"), axis=0, tiled=True)

    def array(rows, columns, dtype=jnp.float32):
        return jax.ShapeDtypeStruct((rows, columns), dtype)

    whole, column, edge = array(byte_rows, width), array(byte_rows, 1), array(1, 2 * width + 256)
    seg_sums, grad_sums, counts, first, last = on_core(
        sums_kernel,
        [whole, whole, column, edge, edge],
        segment_ids,
        segment_ids.reshape(1, byte_rows),
        byte_acts,
        upstream,
    )
    tail, head = shifted(first, seq, -1), shifted(last, seq, 1)
    both, pooled, grad_sums, safe_counts = on_core(
        joined_kernel,
        [array(2 * byte_rows, width, jnp.bfloat16), whole, whole, column],
        segment_ids,
        seg_sums,
        grad_sums,
        counts,
        tail,
        head,
    )
    gathered = ring_gather(both)
    pooled_b = gathered[:byte_rows]
    square_sums = jnp.sum(jnp.square(pooled_b.astype(jnp.float32)), axis=1)
    inv_rms = lax.rsqrt(square_sums / model_width + epsilon)[:, None]

    kept = 144
    sent, rest = block_terms(gathered, weights, inv_rms, width, kept)

    def exchanged(a):
        return lax.all_to_all(a, "tp", split_axis=0, concat_axis=0, tiled=True)

    terms, rest = lax.optimization_barrier((exchanged(sent), rest))
    rest_grad = lax.cond(
        segment_ids[byte_rows - 1] - segment_ids[0] >= kept - 8,
        lambda a: jnp.sum(exchanged(a).astype(jnp.float32), axis=0)[8:],
        lambda a: jnp.zeros((byte_rows - kept + 8, width), jnp.float32),
        rest,
    )
    return on_core(
        functools.partial(last_kernel, model_width),
        array(byte_rows, width, jnp.bfloat16),
        segment_ids,
        segment_ids.reshape(byte_rows, 1),
        terms,
        rest_grad,
        pooled,
        grad_sums,
        safe_counts,
        inv_rms,
        upstream,
        scratch=[pltpu.VMEM((byte_rows, width), jnp.float32)],
    )


def solution(mesh):
    grid = Mesh(mesh.devices.reshape(sizes + (-1,)), seq + ("tp",))
    return jax.shard_map(
        body,
        mesh=grid,
        in_specs=(P(seq, "tp"), P(seq, "tp"), P(seq), P(seq, "tp"), P(seq, "tp")),
        out_specs=P(seq, "tp"),
        check_vma=False,
    )
```

```python
import functools

import jax
import jax.numpy as jnp
from jax import lax
from jax.experimental import pallas as pl
from jax.experimental.pallas import tpu as pltpu
from jax.sharding import Mesh
from jax.sharding import PartitionSpec as P

epsilon = 1e-06
seq = ("y", "x", "core")
sizes = (8, 4, 2)


def shifted(shard, axis, by):
    count = lax.axis_size(axis)
    pairs = [(i, i + by) for i in range(count) if 0 <= i + by < count]
    return lax.ppermute(shard, axis, pairs)


def turned(shard, by):
    count = lax.axis_size("tp")
    return lax.ppermute(shard, "tp", [(i, (i + by) % count) for i in range(count)])


def ring_gather(block):
    count = lax.axis_size("tp")
    me = lax.axis_index("tp")
    rows, width = block.shape
    whole = jnp.zeros((rows, width * count), block.dtype)

    def put(whole, part, row, owner):
        return lax.dynamic_update_slice(whole, part, (row, lax.rem(owner + count, count) * width))

    whole = put(whole, block, 0, me)
    right = left = block
    for step in range(1, count // 2):
        right, left = turned(right, 1), turned(left, -1)
        whole = put(whole, right, 0, me - step)
        whole = put(whole, left, 0, me + step)
    half = rows // 2
    top, bottom = turned(right[:half], 1), turned(left[half:], -1)
    whole = put(whole, top, 0, me + count // 2)
    return put(whole, bottom, half, me + count // 2)


def block_kernel(
    acts_ref, weights_hbm, inv_rms_ref, out_hbm, rest_hbm, weights_ref, turned_ref, mixed_ref, out_ref, rest_ref, sems, out_sems
):
    rows = inv_rms_ref.shape[0]
    hidden = weights_ref.shape[-1]
    blocks, kept, width = out_ref.shape
    copies = [
        [
            pltpu.make_async_copy(
                weights_hbm.at[y, core], weights_ref.at[y, :, :, core], sems.at[y, core]
            )
            for core in range(weights_hbm.shape[1])
        ]
        for y in range(weights_hbm.shape[0])
    ]
    for pair in copies:
        for copy in pair:
            copy.start()
    per_chunk = len(copies) // blocks

    def chunk(k, which):
        return weights_ref[k * per_chunk : (k + 1) * per_chunk, :, which].reshape(width, hidden)

    up_proj = back_proj = jnp.zeros((rows, hidden), jnp.float32)
    for k in range(blocks):
        for pair in copies[k * per_chunk : (k + 1) * per_chunk]:
            for copy in pair:
                copy.wait()
        at = pl.ds(k * width, width)
        own = chunk(k, 0)
        up_proj += jnp.dot(acts_ref[:rows, at], own, preferred_element_type=jnp.float32)
        turned_ref[k] = own.T
        back_proj += jnp.dot(
            acts_ref[rows:, at], chunk(k, 1), preferred_element_type=jnp.float32
        )
    up_proj = up_proj * inv_rms_ref[...]
    sigmoid_up = jax.nn.sigmoid(up_proj)
    grad_hidden = (back_proj * sigmoid_up * (1.0 + up_proj * (1.0 - sigmoid_up))).astype(
        jnp.bfloat16
    )
    product = grad_hidden.astype(jnp.float32) * up_proj
    ones = jnp.ones((16, hidden), jnp.bfloat16)
    dots = jnp.zeros((16, rows), jnp.float32)
    for _ in range(2):
        part = product.astype(jnp.bfloat16)
        product = product - part.astype(jnp.float32)
        dots += lax.dot_general(
            ones, part, (((1,), (1,)), ((), ())), preferred_element_type=jnp.float32
        )
    dots = dots[:4]
    high = dots.astype(jnp.bfloat16).astype(jnp.float32)
    mixed_ref[...] = jnp.zeros_like(mixed_ref)
    mixed_ref[8:, :rows] = jnp.concatenate([high, dots - high], axis=0)
    even = kept - 16
    results = []
    for block in range(blocks):
        term = jnp.dot(grad_hidden, turned_ref[block], preferred_element_type=jnp.float32)
        mixed_ref[:8] = term[even : even + 8]
        out_ref[block, :even] = term[:even].astype(jnp.bfloat16)
        out_ref[block, even:] = mixed_ref[...].astype(jnp.bfloat16)
        rest_ref[block] = term[even:].astype(jnp.bfloat16)
        for i, (here, there) in enumerate(((out_ref, out_hbm), (rest_ref, rest_hbm))):
            results.append(pltpu.make_async_copy(here.at[block], there.at[block], out_sems.at[i, block]))
            results[-1].start()
    for copy in results:
        copy.wait()


def block_terms(gathered, weights, inv_rms, width, kept):
    rows, depth = gathered.shape[0] // 2, gathered.shape[1]
    hidden = weights.shape[1]
    blocks = depth // width
    count_y, count_x, count_core = sizes
    part = depth // (count_y * count_x * count_core)
    return pl.pallas_call(
        block_kernel,
        in_specs=[
            pl.BlockSpec(memory_space=pltpu.VMEM),
            pl.BlockSpec(memory_space=pl.ANY),
            pl.BlockSpec(memory_space=pltpu.VMEM),
        ],
        out_specs=[pl.BlockSpec(memory_space=pltpu.HBM)] * 2,
        out_shape=[
            pltpu.HBM((blocks, kept, width), jnp.bfloat16),
            pltpu.HBM((blocks, rows - kept + 16, width), jnp.bfloat16),
        ],
        scratch_shapes=[
            pltpu.VMEM((count_y, count_x, 2, count_core, part, hidden), jnp.bfloat16),
            pltpu.VMEM((blocks, hidden, width), jnp.bfloat16),
            pltpu.VMEM((16, width), jnp.float32),
            pltpu.VMEM((blocks, kept, width), jnp.bfloat16),
            pltpu.VMEM((blocks, rows - kept + 16, width), jnp.bfloat16),
            pltpu.SemaphoreType.DMA((count_y, count_core)),
            pltpu.SemaphoreType.DMA((2, blocks)),
        ],
        compiler_params=pltpu.CompilerParams(vmem_limit_bytes=40 * 1024 * 1024),
        cost_estimate=pl.CostEstimate(
            flops=6 * rows * depth * hidden,
            bytes_accessed=2 * (2 * rows * depth + 2 * depth * hidden + rows * depth),
            transcendentals=rows * hidden,
        ),
    )(gathered, weights.reshape(count_y, count_core, count_x, 2, part, hidden), inv_rms)


def sums_kernel(ids_ref, ids_row_ref, acts_ref, upstream_ref, seg_ref, grad_ref, count_ref, first_ref, last_ref):
    rows, width = acts_ref.shape
    base_id, last_id = ids_ref[0], ids_ref[rows - 1]
    slot = lax.broadcasted_iota(jnp.int32, (rows, rows), 0)
    member = (slot == ids_row_ref[...] - base_id).astype(jnp.float32)
    member_b = member.astype(jnp.bfloat16)
    seg_ref[...] = jnp.dot(member_b, acts_ref[...], preferred_element_type=jnp.float32)
    grad_ref[...] = jnp.dot(member_b, upstream_ref[...], preferred_element_type=jnp.float32)
    count_ref[...] = jnp.sum(member, axis=1, keepdims=True)
    for edge_ref, at, segment in ((first_ref, 0, base_id), (last_ref, last_id - base_id, last_id)):
        edge_ref[:, :width] = seg_ref[pl.ds(at, 1), :]
        edge_ref[:, width : 2 * width] = grad_ref[pl.ds(at, 1), :]
        count = jnp.sum(jnp.where(slot[:, :1] == at, count_ref[...], 0.0), axis=0, keepdims=True)
        edge_ref[:, 2 * width : 2 * width + 128] = jnp.broadcast_to(count, (1, 128))
        edge_ref[:, 2 * width + 128 :] = jnp.full((1, 128), (segment + 1).astype(jnp.float32))


def joined_kernel(
    ids_ref, seg_ref, grad_ref, count_ref, tail_ref, head_ref, both_ref, pooled_ref, sums_ref, safe_ref
):
    rows, width = seg_ref.shape
    base_id, last_id = ids_ref[0], ids_ref[rows - 1]
    slot = lax.broadcasted_iota(jnp.int32, (rows, 1), 0)

    def pick(edge_ref, at, segment):
        matched = edge_ref[:, 2 * width + 128 : 2 * width + 129] == (segment + 1).astype(jnp.float32)
        return jnp.where((slot == at) & matched, 1.0, 0.0)

    tail_pick = pick(tail_ref, last_id - base_id, last_id)
    head_pick = pick(head_ref, 0, base_id)

    def joined(own_ref, at):
        return own_ref[...] + tail_pick * tail_ref[:, at] + head_pick * head_ref[:, at]

    counts = joined(count_ref, slice(2 * width, 2 * width + 1))
    safe = jnp.maximum(counts, 1.0)
    pooled = joined(seg_ref, slice(0, width)) / safe
    sums = joined(grad_ref, slice(width, 2 * width))
    both_ref[:rows] = pooled.astype(jnp.bfloat16)
    both_ref[rows:] = sums.astype(jnp.bfloat16)
    pooled_ref[...] = pooled
    sums_ref[...] = sums
    safe_ref[...] = safe


def last_kernel(
    model_width,
    ids_ref,
    ids_column_ref,
    terms_ref,
    rest_ref,
    pooled_ref,
    sums_ref,
    safe_ref,
    inv_rms_ref,
    upstream_ref,
    out_ref,
    share_ref,
):
    rows = pooled_ref.shape[0]
    blocks, kept, _ = terms_ref.shape
    even = kept - 16
    norm_grad = terms_ref[0, :even].astype(jnp.float32)
    mixed = terms_ref[0, even:].astype(jnp.float32)
    for block in range(1, blocks):
        norm_grad += terms_ref[block, :even].astype(jnp.float32)
        mixed += terms_ref[block, even:].astype(jnp.float32)
    dots = mixed[8:9, :rows] + mixed[12:13, :rows]
    slot = lax.broadcasted_iota(jnp.int32, (rows, rows), 1)
    diagonal = lax.broadcasted_iota(jnp.int32, (rows, rows), 0) == slot
    norm_dot = jnp.sum(jnp.where(diagonal, dots, 0.0), axis=1, keepdims=True)

    def share(at, norm_grad):
        inv_rms = inv_rms_ref[at]
        normed = pooled_ref[at] * inv_rms
        mean = norm_dot[at] * (1.0 / model_width)
        pooled_grad = sums_ref[at] + inv_rms * (norm_grad - normed * mean)
        share_ref[at] = pooled_grad / safe_ref[at]

    share(slice(0, even), norm_grad)
    share(slice(even, even + 8), mixed[:8])
    share(slice(even + 8, rows), rest_ref[...])
    member = (slot == ids_column_ref[...] - ids_ref[0]).astype(jnp.float32).astype(jnp.bfloat16)
    left = share_ref[...]
    spread = upstream_ref[...].astype(jnp.float32)
    parts = []
    for _ in range(2):
        part = left.astype(jnp.bfloat16)
        left = left - part.astype(jnp.float32)
        parts.append(jnp.dot(member, part, preferred_element_type=jnp.float32))
    out_ref[...] = (spread + (parts[1] + parts[0])).astype(jnp.bfloat16)


def on_core(kernel, out_shape, *operands, scratch=()):
    def whole(a):
        return pl.BlockSpec(a.shape, lambda i: (0,) * len(a.shape))

    return pl.pallas_call(
        kernel,
        grid=(1,),
        in_specs=[pl.BlockSpec(memory_space=pltpu.SMEM)] + [whole(a) for a in operands[1:]],
        out_specs=jax.tree.map(whole, out_shape),
        out_shape=out_shape,
        scratch_shapes=scratch,
        compiler_params=pltpu.CompilerParams(vmem_limit_bytes=24 * 1024 * 1024),
    )(*operands)


def body(byte_acts, upstream, segment_ids, first_weight, second_weight):
    byte_rows, width = byte_acts.shape
    model_width = width * lax.axis_size("tp")
    weights = jnp.concatenate([first_weight, second_weight], axis=0)
    weights = lax.all_gather(weights, "x", axis=0, tiled=True)
    weights = lax.all_gather(weights, ("y", "core"), axis=0, tiled=True)

    def array(rows, columns, dtype=jnp.float32):
        return jax.ShapeDtypeStruct((rows, columns), dtype)

    whole, column, edge = array(byte_rows, width), array(byte_rows, 1), array(1, 2 * width + 256)
    seg_sums, grad_sums, counts, first, last = on_core(
        sums_kernel,
        [whole, whole, column, edge, edge],
        segment_ids,
        segment_ids.reshape(1, byte_rows),
        byte_acts,
        upstream,
    )
    tail, head = shifted(first, seq, -1), shifted(last, seq, 1)
    both, pooled, grad_sums, safe_counts = on_core(
        joined_kernel,
        [array(2 * byte_rows, width, jnp.bfloat16), whole, whole, column],
        segment_ids,
        seg_sums,
        grad_sums,
        counts,
        tail,
        head,
    )
    gathered = ring_gather(both)
    pooled_b = gathered[:byte_rows]
    square_sums = jnp.sum(jnp.square(pooled_b.astype(jnp.float32)), axis=1)
    inv_rms = lax.rsqrt(square_sums / model_width + epsilon)[:, None]

    kept = 144
    sent, rest = block_terms(gathered, weights, inv_rms, width, kept)

    def exchanged(a):
        return lax.all_to_all(a, "tp", split_axis=0, concat_axis=0, tiled=True)

    terms, rest = lax.optimization_barrier((exchanged(sent), rest))
    rest_grad = lax.cond(
        segment_ids[byte_rows - 1] - segment_ids[0] >= kept - 8,
        lambda a: jnp.sum(exchanged(a).astype(jnp.float32), axis=0)[8:],
        lambda a: jnp.zeros((byte_rows - kept + 8, width), jnp.float32),
        rest,
    )
    return on_core(
        functools.partial(last_kernel, model_width),
        array(byte_rows, width, jnp.bfloat16),
        segment_ids,
        segment_ids.reshape(byte_rows, 1),
        terms,
        rest_grad,
        pooled,
        grad_sums,
        safe_counts,
        inv_rms,
        upstream,
        scratch=[pltpu.VMEM((byte_rows, width), jnp.float32)],
    )


def solution(mesh):
    grid = Mesh(mesh.devices.reshape(sizes + (-1,)), seq + ("tp",))
    return jax.shard_map(
        body,
        mesh=grid,
        in_specs=(P(seq, "tp"), P(seq, "tp"), P(seq), P(seq, "tp"), P(seq, "tp")),
        out_specs=P(seq, "tp"),
        check_vma=False,
    )
```

```python
import functools

import jax
import jax.numpy as jnp
from jax import lax
from jax.experimental import pallas as pl
from jax.experimental.pallas import tpu as pltpu
from jax.sharding import Mesh
from jax.sharding import PartitionSpec as P

epsilon = 1e-06
seq = ("y", "x", "core")
sizes = (8, 4, 2)


def shifted(shard, axis, by):
    count = lax.axis_size(axis)
    pairs = [(i, i + by) for i in range(count) if 0 <= i + by < count]
    return lax.ppermute(shard, axis, pairs)


def turned(shard, by):
    count = lax.axis_size("tp")
    return lax.ppermute(shard, "tp", [(i, (i + by) % count) for i in range(count)])


def ring_gather(block):
    count = lax.axis_size("tp")
    me = lax.axis_index("tp")
    rows, width = block.shape
    whole = jnp.zeros((rows, width * count), block.dtype)

    def put(whole, part, row, owner):
        return lax.dynamic_update_slice(whole, part, (row, lax.rem(owner + count, count) * width))

    whole = put(whole, block, 0, me)
    right = left = block
    for step in range(1, count // 2):
        right, left = turned(right, 1), turned(left, -1)
        whole = put(whole, right, 0, me - step)
        whole = put(whole, left, 0, me + step)
    half = rows // 2
    top, bottom = turned(right[:half], 1), turned(left[half:], -1)
    whole = put(whole, top, 0, me + count // 2)
    return put(whole, bottom, half, me + count // 2)


def block_kernel(
    acts_ref, weights_hbm, inv_rms_ref, out_hbm, rest_hbm, weights_ref, turned_ref, mixed_ref, out_ref, rest_ref, sems, out_sems
):
    rows = inv_rms_ref.shape[0]
    hidden = weights_ref.shape[-1]
    blocks, kept, width = out_ref.shape
    copies = [
        [
            pltpu.make_async_copy(
                weights_hbm.at[y, core], weights_ref.at[y, :, :, core], sems.at[y, core]
            )
            for core in range(weights_hbm.shape[1])
        ]
        for y in range(weights_hbm.shape[0])
    ]
    for pair in copies:
        for copy in pair:
            copy.start()
    per_chunk = len(copies) // blocks

    def chunk(k, which):
        return weights_ref[k * per_chunk : (k + 1) * per_chunk, :, which].reshape(width, hidden)

    up_proj = back_proj = jnp.zeros((rows, hidden), jnp.float32)
    for k in range(blocks):
        for pair in copies[k * per_chunk : (k + 1) * per_chunk]:
            for copy in pair:
                copy.wait()
        at = pl.ds(k * width, width)
        own = chunk(k, 0)
        up_proj += jnp.dot(acts_ref[:rows, at], own, preferred_element_type=jnp.float32)
        turned_ref[k] = own.T
        back_proj += jnp.dot(
            acts_ref[rows:, at], chunk(k, 1), preferred_element_type=jnp.float32
        )
    up_proj = up_proj * inv_rms_ref[...]
    sigmoid_up = jax.nn.sigmoid(up_proj)
    grad_hidden = (back_proj * sigmoid_up * (1.0 + up_proj * (1.0 - sigmoid_up))).astype(
        jnp.bfloat16
    )
    product = grad_hidden.astype(jnp.float32) * up_proj
    ones = jnp.ones((16, hidden), jnp.bfloat16)
    dots = jnp.zeros((16, rows), jnp.float32)
    for _ in range(2):
        part = product.astype(jnp.bfloat16)
        product = product - part.astype(jnp.float32)
        dots += lax.dot_general(
            ones, part, (((1,), (1,)), ((), ())), preferred_element_type=jnp.float32
        )
    dots = dots[:4]
    high = dots.astype(jnp.bfloat16).astype(jnp.float32)
    mixed_ref[...] = jnp.zeros_like(mixed_ref)
    mixed_ref[8:, :rows] = jnp.concatenate([high, dots - high], axis=0)
    even = kept - 16
    results = []
    for block in range(blocks):
        term = jnp.dot(grad_hidden, turned_ref[block], preferred_element_type=jnp.float32)
        mixed_ref[:8] = term[even : even + 8]
        out_ref[block, :even] = term[:even].astype(jnp.bfloat16)
        out_ref[block, even:] = mixed_ref[...].astype(jnp.bfloat16)
        rest_ref[block] = term[even:].astype(jnp.bfloat16)
        for i, (here, there) in enumerate(((out_ref, out_hbm), (rest_ref, rest_hbm))):
            results.append(pltpu.make_async_copy(here.at[block], there.at[block], out_sems.at[i, block]))
            results[-1].start()
    for copy in results:
        copy.wait()


def block_terms(gathered, weights, inv_rms, width, kept):
    rows, depth = gathered.shape[0] // 2, gathered.shape[1]
    hidden = weights.shape[1]
    blocks = depth // width
    count_y, count_x, count_core = sizes
    part = depth // (count_y * count_x * count_core)
    return pl.pallas_call(
        block_kernel,
        in_specs=[
            pl.BlockSpec(memory_space=pltpu.VMEM),
            pl.BlockSpec(memory_space=pl.ANY),
            pl.BlockSpec(memory_space=pltpu.VMEM),
        ],
        out_specs=[pl.BlockSpec(memory_space=pltpu.HBM)] * 2,
        out_shape=[
            pltpu.HBM((blocks, kept, width), jnp.bfloat16),
            pltpu.HBM((blocks, rows - kept + 16, width), jnp.bfloat16),
        ],
        scratch_shapes=[
            pltpu.VMEM((count_y, count_x, 2, count_core, part, hidden), jnp.bfloat16),
            pltpu.VMEM((blocks, hidden, width), jnp.bfloat16),
            pltpu.VMEM((16, width), jnp.float32),
            pltpu.VMEM((blocks, kept, width), jnp.bfloat16),
            pltpu.VMEM((blocks, rows - kept + 16, width), jnp.bfloat16),
            pltpu.SemaphoreType.DMA((count_y, count_core)),
            pltpu.SemaphoreType.DMA((2, blocks)),
        ],
        compiler_params=pltpu.CompilerParams(vmem_limit_bytes=40 * 1024 * 1024),
        cost_estimate=pl.CostEstimate(
            flops=6 * rows * depth * hidden,
            bytes_accessed=2 * (2 * rows * depth + 2 * depth * hidden + rows * depth),
            transcendentals=rows * hidden,
        ),
    )(gathered, weights.reshape(count_y, count_core, count_x, 2, part, hidden), inv_rms)


def sums_kernel(ids_ref, ids_row_ref, acts_ref, upstream_ref, seg_ref, grad_ref, count_ref, first_ref, last_ref):
    rows, width = acts_ref.shape
    base_id, last_id = ids_ref[0], ids_ref[rows - 1]
    slot = lax.broadcasted_iota(jnp.int32, (rows, rows), 0)
    member = (slot == ids_row_ref[...] - base_id).astype(jnp.float32)
    member_b = member.astype(jnp.bfloat16)
    seg_ref[...] = jnp.dot(member_b, acts_ref[...], preferred_element_type=jnp.float32)
    grad_ref[...] = jnp.dot(member_b, upstream_ref[...], preferred_element_type=jnp.float32)
    count_ref[...] = jnp.sum(member, axis=1, keepdims=True)
    for edge_ref, at, segment in ((first_ref, 0, base_id), (last_ref, last_id - base_id, last_id)):
        edge_ref[:, :width] = seg_ref[pl.ds(at, 1), :]
        edge_ref[:, width : 2 * width] = grad_ref[pl.ds(at, 1), :]
        count = jnp.sum(jnp.where(slot[:, :1] == at, count_ref[...], 0.0), axis=0, keepdims=True)
        edge_ref[:, 2 * width : 2 * width + 128] = jnp.broadcast_to(count, (1, 128))
        edge_ref[:, 2 * width + 128 :] = jnp.full((1, 128), (segment + 1).astype(jnp.float32))


def joined_kernel(
    ids_ref, seg_ref, grad_ref, count_ref, tail_ref, head_ref, both_ref, pooled_ref, sums_ref, safe_ref
):
    rows, width = seg_ref.shape
    base_id, last_id = ids_ref[0], ids_ref[rows - 1]
    slot = lax.broadcasted_iota(jnp.int32, (rows, 1), 0)

    def pick(edge_ref, at, segment):
        matched = edge_ref[:, 2 * width + 128 : 2 * width + 129] == (segment + 1).astype(jnp.float32)
        return jnp.where((slot == at) & matched, 1.0, 0.0)

    tail_pick = pick(tail_ref, last_id - base_id, last_id)
    head_pick = pick(head_ref, 0, base_id)

    def joined(own_ref, at):
        return own_ref[...] + tail_pick * tail_ref[:, at] + head_pick * head_ref[:, at]

    counts = joined(count_ref, slice(2 * width, 2 * width + 1))
    safe = jnp.maximum(counts, 1.0)
    pooled = joined(seg_ref, slice(0, width)) / safe
    sums = joined(grad_ref, slice(width, 2 * width))
    both_ref[:rows] = pooled.astype(jnp.bfloat16)
    both_ref[rows:] = sums.astype(jnp.bfloat16)
    pooled_ref[...] = pooled
    sums_ref[...] = sums
    safe_ref[...] = safe


def membership(ids_ref, ids_column_ref, rows):
    slot = lax.broadcasted_iota(jnp.int32, (rows, rows), 1)
    return slot == ids_column_ref[...] - ids_ref[0]


def spread(member, share):
    member = member.astype(jnp.float32).astype(jnp.bfloat16)
    high = share.astype(jnp.bfloat16)
    low = (share - high.astype(jnp.float32)).astype(jnp.bfloat16)
    return jnp.dot(member, low, preferred_element_type=jnp.float32) + jnp.dot(
        member, high, preferred_element_type=jnp.float32
    )


def ahead_kernel(
    model_width,
    ids_ref,
    ids_column_ref,
    pooled_ref,
    sums_ref,
    safe_ref,
    inv_rms_ref,
    upstream_ref,
    known_ref,
    slope_ref,
    scale_ref,
):
    member = membership(ids_ref, ids_column_ref, pooled_ref.shape[0])
    scale = inv_rms_ref[...] / safe_ref[...]
    known_ref[...] = upstream_ref[...].astype(jnp.float32) + spread(member, sums_ref[...] / safe_ref[...])
    slope_ref[...] = spread(member, pooled_ref[...] * (scale * inv_rms_ref[...] * (1.0 / model_width)))
    scale_ref[...] = scale


def last_kernel(
    ids_ref, ids_column_ref, terms_ref, rest_ref, known_ref, slope_ref, scale_ref, out_ref, share_ref
):
    rows = known_ref.shape[0]
    blocks, kept, _ = terms_ref.shape
    even = kept - 16
    norm_grad = terms_ref[0, :even].astype(jnp.float32)
    mixed = terms_ref[0, even:].astype(jnp.float32)
    for block in range(1, blocks):
        norm_grad += terms_ref[block, :even].astype(jnp.float32)
        mixed += terms_ref[block, even:].astype(jnp.float32)
    share_ref[:even] = norm_grad * scale_ref[:even]
    share_ref[even : even + 8] = mixed[:8] * scale_ref[even : even + 8]
    share_ref[even + 8 :] = rest_ref[...] * scale_ref[even + 8 :]
    member = membership(ids_ref, ids_column_ref, rows)
    dots = mixed[8:9, :rows] + mixed[12:13, :rows]
    norm_dot = jnp.sum(jnp.where(member, dots, 0.0), axis=1, keepdims=True)
    out_ref[...] = (known_ref[...] - slope_ref[...] * norm_dot + spread(member, share_ref[...])).astype(
        jnp.bfloat16
    )


def on_core(kernel, out_shape, *operands, scratch=()):
    def whole(a):
        return pl.BlockSpec(a.shape, lambda i: (0,) * len(a.shape))

    return pl.pallas_call(
        kernel,
        grid=(1,),
        in_specs=[pl.BlockSpec(memory_space=pltpu.SMEM)] + [whole(a) for a in operands[1:]],
        out_specs=jax.tree.map(whole, out_shape),
        out_shape=out_shape,
        scratch_shapes=scratch,
        compiler_params=pltpu.CompilerParams(vmem_limit_bytes=24 * 1024 * 1024),
    )(*operands)


def body(byte_acts, upstream, segment_ids, first_weight, second_weight):
    byte_rows, width = byte_acts.shape
    model_width = width * lax.axis_size("tp")
    weights = jnp.concatenate([first_weight, second_weight], axis=0)
    weights = lax.all_gather(weights, "x", axis=0, tiled=True)
    weights = lax.all_gather(weights, ("y", "core"), axis=0, tiled=True)

    def array(rows, columns, dtype=jnp.float32):
        return jax.ShapeDtypeStruct((rows, columns), dtype)

    whole, column, edge = array(byte_rows, width), array(byte_rows, 1), array(1, 2 * width + 256)
    seg_sums, grad_sums, counts, first, last = on_core(
        sums_kernel,
        [whole, whole, column, edge, edge],
        segment_ids,
        segment_ids.reshape(1, byte_rows),
        byte_acts,
        upstream,
    )
    tail, head = shifted(first, seq, -1), shifted(last, seq, 1)
    both, pooled, grad_sums, safe_counts = on_core(
        joined_kernel,
        [array(2 * byte_rows, width, jnp.bfloat16), whole, whole, column],
        segment_ids,
        seg_sums,
        grad_sums,
        counts,
        tail,
        head,
    )
    gathered = ring_gather(both)
    pooled_b = gathered[:byte_rows]
    square_sums = jnp.sum(jnp.square(pooled_b.astype(jnp.float32)), axis=1)
    inv_rms = lax.rsqrt(square_sums / model_width + epsilon)[:, None]

    ids_column = segment_ids.reshape(byte_rows, 1)
    known, slope, scale = on_core(
        functools.partial(ahead_kernel, model_width),
        [whole, whole, column],
        segment_ids,
        ids_column,
        pooled,
        grad_sums,
        safe_counts,
        inv_rms,
        upstream,
    )

    kept = 144
    sent, rest = block_terms(gathered, weights, inv_rms, width, kept)

    def exchanged(a):
        return lax.all_to_all(a, "tp", split_axis=0, concat_axis=0, tiled=True)

    terms, rest = lax.optimization_barrier((exchanged(sent), rest))
    rest_grad = lax.cond(
        segment_ids[byte_rows - 1] - segment_ids[0] >= kept - 8,
        lambda a: jnp.sum(exchanged(a).astype(jnp.float32), axis=0)[8:],
        lambda a: jnp.zeros((byte_rows - kept + 8, width), jnp.float32),
        rest,
    )
    return on_core(
        last_kernel,
        array(byte_rows, width, jnp.bfloat16),
        segment_ids,
        ids_column,
        terms,
        rest_grad,
        known,
        slope,
        scale,
        scratch=[pltpu.VMEM((byte_rows, width), jnp.float32)],
    )


def solution(mesh):
    grid = Mesh(mesh.devices.reshape(sizes + (-1,)), seq + ("tp",))
    return jax.shard_map(
        body,
        mesh=grid,
        in_specs=(P(seq, "tp"), P(seq, "tp"), P(seq), P(seq, "tp"), P(seq, "tp")),
        out_specs=P(seq, "tp"),
        check_vma=False,
    )
```

```python
import functools

import jax
import jax.numpy as jnp
from jax import lax
from jax.experimental import pallas as pl
from jax.experimental.pallas import tpu as pltpu
from jax.sharding import Mesh
from jax.sharding import PartitionSpec as P

epsilon = 1e-06
seq = ("y", "x", "core")
sizes = (8, 4, 2)


def shifted(shard, axis, by):
    count = lax.axis_size(axis)
    pairs = [(i, i + by) for i in range(count) if 0 <= i + by < count]
    return lax.ppermute(shard, axis, pairs)


def turned(shard, by):
    count = lax.axis_size("tp")
    return lax.ppermute(shard, "tp", [(i, (i + by) % count) for i in range(count)])


def ring_gather(block):
    count = lax.axis_size("tp")
    me = lax.axis_index("tp")
    rows, width = block.shape
    whole = jnp.zeros((rows, width * count), block.dtype)

    def put(whole, part, row, owner):
        return lax.dynamic_update_slice(whole, part, (row, lax.rem(owner + count, count) * width))

    whole = put(whole, block, 0, me)
    right = left = block
    for step in range(1, count // 2):
        right, left = turned(right, 1), turned(left, -1)
        whole = put(whole, right, 0, me - step)
        whole = put(whole, left, 0, me + step)
    half = rows // 2
    top, bottom = turned(right[:half], 1), turned(left[half:], -1)
    whole = put(whole, top, 0, me + count // 2)
    return put(whole, bottom, half, me + count // 2)


def block_kernel(
    acts_ref, weights_hbm, inv_rms_ref, out_hbm, rest_hbm, weights_ref, turned_ref, mixed_ref, out_ref, rest_ref, sems, out_sems
):
    rows = inv_rms_ref.shape[0]
    hidden = weights_ref.shape[-1]
    blocks, kept, width = out_ref.shape
    copies = [
        [
            pltpu.make_async_copy(
                weights_hbm.at[y, core], weights_ref.at[y, :, :, core], sems.at[y, core]
            )
            for core in range(weights_hbm.shape[1])
        ]
        for y in range(weights_hbm.shape[0])
    ]
    for pair in copies:
        for copy in pair:
            copy.start()
    per_chunk = len(copies) // blocks

    def chunk(k, which):
        return weights_ref[k * per_chunk : (k + 1) * per_chunk, :, which].reshape(width, hidden)

    up_proj = back_proj = jnp.zeros((rows, hidden), jnp.float32)
    for k in range(blocks):
        for pair in copies[k * per_chunk : (k + 1) * per_chunk]:
            for copy in pair:
                copy.wait()
        at = pl.ds(k * width, width)
        own = chunk(k, 0)
        up_proj += jnp.dot(acts_ref[:rows, at], own, preferred_element_type=jnp.float32)
        turned_ref[k] = own.T
        back_proj += jnp.dot(
            acts_ref[rows:, at], chunk(k, 1), preferred_element_type=jnp.float32
        )
    up_proj = up_proj * inv_rms_ref[...]
    sigmoid_up = jax.nn.sigmoid(up_proj)
    grad_hidden = (back_proj * sigmoid_up * (1.0 + up_proj * (1.0 - sigmoid_up))).astype(
        jnp.bfloat16
    )
    product = grad_hidden.astype(jnp.float32) * up_proj
    ones = jnp.ones((16, hidden), jnp.bfloat16)
    dots = jnp.zeros((16, rows), jnp.float32)
    for _ in range(2):
        part = product.astype(jnp.bfloat16)
        product = product - part.astype(jnp.float32)
        dots += lax.dot_general(
            ones, part, (((1,), (1,)), ((), ())), preferred_element_type=jnp.float32
        )
    dots = dots[:4]
    high = dots.astype(jnp.bfloat16).astype(jnp.float32)
    mixed_ref[...] = jnp.zeros_like(mixed_ref)
    mixed_ref[8:, :rows] = jnp.concatenate([high, dots - high], axis=0)
    even = kept - 16
    results = []
    for block in range(blocks):
        term = jnp.dot(grad_hidden, turned_ref[block], preferred_element_type=jnp.float32)
        mixed_ref[:8] = term[even : even + 8]
        out_ref[block, :even] = term[:even].astype(jnp.bfloat16)
        out_ref[block, even:] = mixed_ref[...].astype(jnp.bfloat16)
        rest_ref[block] = term[even:].astype(jnp.bfloat16)
        for i, (here, there) in enumerate(((out_ref, out_hbm), (rest_ref, rest_hbm))):
            results.append(pltpu.make_async_copy(here.at[block], there.at[block], out_sems.at[i, block]))
            results[-1].start()
    for copy in results:
        copy.wait()


def block_terms(gathered, weights, inv_rms, width, kept):
    rows, depth = gathered.shape[0] // 2, gathered.shape[1]
    hidden = weights.shape[1]
    blocks = depth // width
    count_y, count_x, count_core = sizes
    part = depth // (count_y * count_x * count_core)
    return pl.pallas_call(
        block_kernel,
        in_specs=[
            pl.BlockSpec(memory_space=pltpu.VMEM),
            pl.BlockSpec(memory_space=pl.ANY),
            pl.BlockSpec(memory_space=pltpu.VMEM),
        ],
        out_specs=[pl.BlockSpec(memory_space=pltpu.HBM)] * 2,
        out_shape=[
            pltpu.HBM((blocks, kept, width), jnp.bfloat16),
            pltpu.HBM((blocks, rows - kept + 16, width), jnp.bfloat16),
        ],
        scratch_shapes=[
            pltpu.VMEM((count_y, count_x, 2, count_core, part, hidden), jnp.bfloat16),
            pltpu.VMEM((blocks, hidden, width), jnp.bfloat16),
            pltpu.VMEM((16, width), jnp.float32),
            pltpu.VMEM((blocks, kept, width), jnp.bfloat16),
            pltpu.VMEM((blocks, rows - kept + 16, width), jnp.bfloat16),
            pltpu.SemaphoreType.DMA((count_y, count_core)),
            pltpu.SemaphoreType.DMA((2, blocks)),
        ],
        compiler_params=pltpu.CompilerParams(vmem_limit_bytes=40 * 1024 * 1024),
        cost_estimate=pl.CostEstimate(
            flops=6 * rows * depth * hidden,
            bytes_accessed=2 * (2 * rows * depth + 2 * depth * hidden + rows * depth),
            transcendentals=rows * hidden,
        ),
    )(gathered, weights.reshape(count_y, count_core, count_x, 2, part, hidden), inv_rms)


def sums_kernel(ids_ref, ids_row_ref, acts_ref, upstream_ref, seg_ref, grad_ref, count_ref, first_ref, last_ref):
    rows, width = acts_ref.shape
    base_id, last_id = ids_ref[0], ids_ref[rows - 1]
    slot = lax.broadcasted_iota(jnp.int32, (rows, rows), 0)
    member = (slot == ids_row_ref[...] - base_id).astype(jnp.float32)
    member_b = member.astype(jnp.bfloat16)
    seg_ref[...] = jnp.dot(member_b, acts_ref[...], preferred_element_type=jnp.float32)
    grad_ref[...] = jnp.dot(member_b, upstream_ref[...], preferred_element_type=jnp.float32)
    count_ref[...] = jnp.sum(member, axis=1, keepdims=True)
    for edge_ref, at, segment in ((first_ref, 0, base_id), (last_ref, last_id - base_id, last_id)):
        edge_ref[:, :width] = seg_ref[pl.ds(at, 1), :]
        edge_ref[:, width : 2 * width] = grad_ref[pl.ds(at, 1), :]
        count = jnp.sum(jnp.where(slot[:, :1] == at, count_ref[...], 0.0), axis=0, keepdims=True)
        edge_ref[:, 2 * width : 2 * width + 128] = jnp.broadcast_to(count, (1, 128))
        edge_ref[:, 2 * width + 128 :] = jnp.full((1, 128), (segment + 1).astype(jnp.float32))


def joined_kernel(
    ids_ref, seg_ref, grad_ref, count_ref, tail_ref, head_ref, both_ref, pooled_ref, sums_ref, safe_ref
):
    rows, width = seg_ref.shape
    base_id, last_id = ids_ref[0], ids_ref[rows - 1]
    slot = lax.broadcasted_iota(jnp.int32, (rows, 1), 0)

    def pick(edge_ref, at, segment):
        matched = edge_ref[:, 2 * width + 128 : 2 * width + 129] == (segment + 1).astype(jnp.float32)
        return jnp.where((slot == at) & matched, 1.0, 0.0)

    tail_pick = pick(tail_ref, last_id - base_id, last_id)
    head_pick = pick(head_ref, 0, base_id)

    def joined(own_ref, at):
        return own_ref[...] + tail_pick * tail_ref[:, at] + head_pick * head_ref[:, at]

    counts = joined(count_ref, slice(2 * width, 2 * width + 1))
    safe = jnp.maximum(counts, 1.0)
    pooled = joined(seg_ref, slice(0, width)) / safe
    sums = joined(grad_ref, slice(width, 2 * width))
    both_ref[:rows] = pooled.astype(jnp.bfloat16)
    both_ref[rows:] = sums.astype(jnp.bfloat16)
    pooled_ref[...] = pooled
    sums_ref[...] = sums
    safe_ref[...] = safe


def stack_kernel(first_hbm, second_hbm, out_hbm, sems):
    rows = first_hbm.shape[0]
    copies = [
        pltpu.make_async_copy(first_hbm, out_hbm.at[pl.ds(0, rows)], sems.at[0]),
        pltpu.make_async_copy(second_hbm, out_hbm.at[pl.ds(rows, rows)], sems.at[1]),
    ]
    for copy in copies:
        copy.start()
    for copy in copies:
        copy.wait()


def membership(ids_ref, ids_column_ref, rows):
    slot = lax.broadcasted_iota(jnp.int32, (rows, rows), 1)
    return slot == ids_column_ref[...] - ids_ref[0]


def spread(member, share):
    member = member.astype(jnp.float32).astype(jnp.bfloat16)
    high = share.astype(jnp.bfloat16)
    low = (share - high.astype(jnp.float32)).astype(jnp.bfloat16)
    return jnp.dot(member, low, preferred_element_type=jnp.float32) + jnp.dot(
        member, high, preferred_element_type=jnp.float32
    )


def ahead_kernel(
    model_width,
    ids_ref,
    ids_column_ref,
    pooled_ref,
    sums_ref,
    safe_ref,
    inv_rms_ref,
    upstream_ref,
    known_ref,
    slope_ref,
    scale_ref,
):
    member = membership(ids_ref, ids_column_ref, pooled_ref.shape[0])
    scale = inv_rms_ref[...] / safe_ref[...]
    known_ref[...] = upstream_ref[...].astype(jnp.float32) + spread(member, sums_ref[...] / safe_ref[...])
    slope_ref[...] = spread(member, pooled_ref[...] * (scale * inv_rms_ref[...] * (1.0 / model_width)))
    scale_ref[...] = scale


def last_kernel(
    ids_ref, ids_column_ref, terms_ref, rest_ref, known_ref, slope_ref, scale_ref, out_ref, share_ref
):
    rows = known_ref.shape[0]
    blocks, kept, _ = terms_ref.shape
    even = kept - 16
    norm_grad = terms_ref[0, :even].astype(jnp.float32)
    mixed = terms_ref[0, even:].astype(jnp.float32)
    for block in range(1, blocks):
        norm_grad += terms_ref[block, :even].astype(jnp.float32)
        mixed += terms_ref[block, even:].astype(jnp.float32)
    share_ref[:even] = norm_grad * scale_ref[:even]
    share_ref[even : even + 8] = mixed[:8] * scale_ref[even : even + 8]
    share_ref[even + 8 :] = rest_ref[...] * scale_ref[even + 8 :]
    member = membership(ids_ref, ids_column_ref, rows)
    dots = mixed[8:9, :rows] + mixed[12:13, :rows]
    norm_dot = jnp.sum(jnp.where(member, dots, 0.0), axis=1, keepdims=True)
    out_ref[...] = (known_ref[...] - slope_ref[...] * norm_dot + spread(member, share_ref[...])).astype(
        jnp.bfloat16
    )


def on_core(kernel, out_shape, *operands, scratch=()):
    def whole(a):
        return pl.BlockSpec(a.shape, lambda i: (0,) * len(a.shape))

    return pl.pallas_call(
        kernel,
        grid=(1,),
        in_specs=[pl.BlockSpec(memory_space=pltpu.SMEM)] + [whole(a) for a in operands[1:]],
        out_specs=jax.tree.map(whole, out_shape),
        out_shape=out_shape,
        scratch_shapes=scratch,
        compiler_params=pltpu.CompilerParams(vmem_limit_bytes=24 * 1024 * 1024),
    )(*operands)


def body(byte_acts, upstream, segment_ids, first_weight, second_weight):
    byte_rows, width = byte_acts.shape
    model_width = width * lax.axis_size("tp")
    weights = pl.pallas_call(
        stack_kernel,
        in_specs=[pl.BlockSpec(memory_space=pltpu.HBM)] * 2,
        out_specs=pl.BlockSpec(memory_space=pltpu.HBM),
        out_shape=pltpu.HBM((2 * first_weight.shape[0], first_weight.shape[1]), first_weight.dtype),
        scratch_shapes=[pltpu.SemaphoreType.DMA((2,))],
    )(first_weight, second_weight)
    weights = lax.all_gather(weights, "x", axis=0, tiled=True)
    weights = lax.all_gather(weights, ("y", "core"), axis=0, tiled=True)

    def array(rows, columns, dtype=jnp.float32):
        return jax.ShapeDtypeStruct((rows, columns), dtype)

    whole, column, edge = array(byte_rows, width), array(byte_rows, 1), array(1, 2 * width + 256)
    seg_sums, grad_sums, counts, first, last = on_core(
        sums_kernel,
        [whole, whole, column, edge, edge],
        segment_ids,
        segment_ids.reshape(1, byte_rows),
        byte_acts,
        upstream,
    )
    tail, head = shifted(first, seq, -1), shifted(last, seq, 1)
    both, pooled, grad_sums, safe_counts = on_core(
        joined_kernel,
        [array(2 * byte_rows, width, jnp.bfloat16), whole, whole, column],
        segment_ids,
        seg_sums,
        grad_sums,
        counts,
        tail,
        head,
    )
    gathered = ring_gather(both)
    pooled_b = gathered[:byte_rows]
    square_sums = jnp.sum(jnp.square(pooled_b.astype(jnp.float32)), axis=1)
    inv_rms = lax.rsqrt(square_sums / model_width + epsilon)[:, None]

    ids_column = segment_ids.reshape(byte_rows, 1)
    known, slope, scale = on_core(
        functools.partial(ahead_kernel, model_width),
        [whole, whole, column],
        segment_ids,
        ids_column,
        pooled,
        grad_sums,
        safe_counts,
        inv_rms,
        upstream,
    )

    kept = 144
    sent, rest = block_terms(gathered, weights, inv_rms, width, kept)

    def exchanged(a):
        return lax.all_to_all(a, "tp", split_axis=0, concat_axis=0, tiled=True)

    terms, rest = lax.optimization_barrier((exchanged(sent), rest))
    rest_grad = lax.cond(
        segment_ids[byte_rows - 1] - segment_ids[0] >= kept - 8,
        lambda a: jnp.sum(exchanged(a).astype(jnp.float32), axis=0)[8:],
        lambda a: jnp.zeros((byte_rows - kept + 8, width), jnp.float32),
        rest,
    )
    return on_core(
        last_kernel,
        array(byte_rows, width, jnp.bfloat16),
        segment_ids,
        ids_column,
        terms,
        rest_grad,
        known,
        slope,
        scale,
        scratch=[pltpu.VMEM((byte_rows, width), jnp.float32)],
    )


def solution(mesh):
    grid = Mesh(mesh.devices.reshape(sizes + (-1,)), seq + ("tp",))
    return jax.shard_map(
        body,
        mesh=grid,
        in_specs=(P(seq, "tp"), P(seq, "tp"), P(seq), P(seq, "tp"), P(seq, "tp")),
        out_specs=P(seq, "tp"),
        check_vma=False,
    )
```
